512 devices in a mesh: seq: 128 (over z, y_lo, x, core), dp: 4 (over y_hi).
Axes of the slice: x: 4, y: 8 (y_hi: 4, y_lo: 2; y = y_hi * 2 + y_lo), z: 8, core: 2. Of those that a mesh axis runs over, the one named last changes fastest.
Arguments:
- values: bfloat16 [4, 16384, 4096], P('dp', 'seq'), may hold values from -6 to 6
- cotangent: bfloat16 [4, 16384, 4096], P('dp', 'seq'), may hold values from -6 to 6
- long_filter: bfloat16 [4096, 16384], P(('seq', 'dp')), may hold values from -2 to 2
- bypass: bfloat16 [4096], P(('seq', 'dp')), may hold values from 0.25 to 2
Outputs:
- grad_values: bfloat16 [4, 16384, 4096], P('dp', 'seq')
- grad_filter: float32 [4096, 16384], P(('seq', 'dp'))
- grad_bypass: float32 [4096], P(('seq', 'dp'))
The draws below stay inside these ranges and needn't reach their ends.
All inputs are finite; a program needn't handle non-finite values.
Results may differ from the reference program's by a relative error of at most 0.01.
Values may be sent and summed in bfloat16 or wider, within the bound.
A program may use at most 128 MiB of HBM per device.

```python
import math
import jax
import jax.numpy as jnp
from jax import lax

C = 4096
LENGTH = 16384
SEQS = 4


def draw_long_filter(key, part):
    key = jax.random.fold_in(key, 11)
    reach_key, noise_key = jax.random.split(key)
    reach_low = math.log(16.0)
    reach_high = math.log(LENGTH * 4.0)
    reach = jnp.exp(jax.random.uniform(reach_key, (C, 1), jnp.float32, reach_low, reach_high))
    lags = jnp.arange(LENGTH, dtype=jnp.float32)[None, :]
    envelope = jnp.exp(-lags / reach) * jnp.sqrt(2.0 / reach + 1.0 / LENGTH)
    noise = jnp.clip(jax.random.normal(noise_key, (C, LENGTH), jnp.float32), -4.0, 4.0)
    return (noise * envelope).astype(jnp.bfloat16)


def block_scale(key, dims, cuts, smallest, largest):
    loudness = 1.0
    for axis_at, blocks in cuts:
        draws = jax.random.uniform(jax.random.fold_in(jax.random.fold_in(key, 6), axis_at), (blocks,), jnp.float32, smallest / len(cuts), largest / len(cuts))
        loudness = loudness * jnp.repeat(jnp.exp(draws), dims[axis_at] // blocks).reshape((-1,) + (1,) * (len(dims) - 1 - axis_at))
    return loudness


def scatter_about(own_key, extent, width, most, cuts=(), held_as=jnp.bfloat16):
    factor_of = block_scale(own_key, extent, cuts, -0.22, 0.18) if cuts else 1.0
    values = jax.random.normal(own_key, extent, jnp.float32) * width * factor_of
    return jnp.minimum(jnp.maximum(values, -most), most).astype(held_as)


def setup_inputs(seed: int = 0) -> dict:
    key_of = jax.random.split(jax.random.key(seed), 5)
    return {
        "values": scatter_about(key_of[0], (SEQS, LENGTH, C), 1.0, 6.0, ((0, 4), (1, 128))),
        "cotangent": scatter_about(key_of[1], (SEQS, LENGTH, C), 1.0, 6.0, ((0, 4), (1, 128))),
        "long_filter": draw_long_filter(jax.random.fold_in(key_of[4], 71), 0),
        "bypass": jnp.clip(jnp.exp(math.log(2.0) - 2.0794415 * jax.random.uniform(key_of[3], (C,), jnp.float32) ** block_scale(key_of[3], (C,), ((0, 512),), -0.2, 0.2)), 0.25, 2.0).astype(jnp.bfloat16),
    }


split_radix = 256

def dft_table(points, orient):
    positions = jnp.arange(points, dtype=jnp.int32)
    product = positions[:, None] * positions[None, :] % points
    angles = 2.0 * math.pi / points * product.astype(jnp.float32)
    return (jnp.cos(angles).astype(jnp.bfloat16), (orient * jnp.sin(angles)).astype(jnp.bfloat16))

def twiddle(rows_count, cols_count, points, orient):
    row_index = jnp.arange(rows_count, dtype=jnp.int32)[:, None]
    col_index = jnp.arange(cols_count, dtype=jnp.int32)[None, :]
    angles = 2.0 * math.pi / points * (row_index * col_index % points).astype(jnp.float32)
    return (jnp.cos(angles), orient * jnp.sin(angles))

def contract(form, table, data):
    return jnp.einsum(form, table.astype(jnp.float32), data.astype(jnp.float32), precision=lax.Precision.HIGHEST)

def is_direct(points):
    return points <= 128 or points % split_radix != 0

def forward(real_part, imag_part):
    points = real_part.shape[-1]
    leading = real_part.shape[:-1]
    if is_direct(points):
        table_real, table_imag = dft_table(points, -1.0)
        out_real = contract('nk,...n->...k', table_real, real_part)
        out_imag = contract('nk,...n->...k', table_imag, real_part)
        if imag_part is not None:
            out_real = out_real - contract('nk,...n->...k', table_imag, imag_part)
            out_imag = out_imag + contract('nk,...n->...k', table_real, imag_part)
        return (out_real.astype(jnp.bfloat16), out_imag.astype(jnp.bfloat16))
    inner_points = points // split_radix
    blocked = leading + (split_radix, inner_points)
    table_real, table_imag = dft_table(split_radix, -1.0)
    split_real = real_part.reshape(blocked)
    section_real = contract('ak,...ab->...kb', table_real, split_real)
    section_imag = contract('ak,...ab->...kb', table_imag, split_real)
    if imag_part is not None:
        split_imag = imag_part.reshape(blocked)
        section_real = section_real - contract('ak,...ab->...kb', table_imag, split_imag)
        section_imag = section_imag + contract('ak,...ab->...kb', table_real, split_imag)
    turn_real, turn_imag = twiddle(split_radix, inner_points, points, -1.0)
    moved_real = (section_real * turn_real - section_imag * turn_imag).astype(jnp.bfloat16)
    moved_imag = (section_real * turn_imag + section_imag * turn_real).astype(jnp.bfloat16)
    out_real, out_imag = forward(moved_real, moved_imag)
    return (out_real.reshape(leading + (points,)), out_imag.reshape(leading + (points,)))

def inverse(real_part, imag_part, keep_imag):
    points = real_part.shape[-1]
    leading = real_part.shape[:-1]
    if is_direct(points):
        table_real, table_imag = dft_table(points, 1.0)
        out_real = contract('nk,...n->...k', table_real, real_part) - contract('nk,...n->...k', table_imag, imag_part)
        if not keep_imag:
            return (out_real, None)
        out_imag = contract('nk,...n->...k', table_imag, real_part) + contract('nk,...n->...k', table_real, imag_part)
        return (out_real, out_imag)
    inner_points = points // split_radix
    blocked = leading + (split_radix, inner_points)
    inner_real, inner_imag = inverse(real_part.reshape(blocked), imag_part.reshape(blocked), True)
    turn_real, turn_imag = twiddle(split_radix, inner_points, points, 1.0)
    moved_real = (inner_real * turn_real - inner_imag * turn_imag).astype(jnp.bfloat16)
    moved_imag = (inner_real * turn_imag + inner_imag * turn_real).astype(jnp.bfloat16)
    table_real, table_imag = dft_table(split_radix, 1.0)
    out_real = contract('ka,...kb->...ab', table_real, moved_real) - contract('ka,...kb->...ab', table_imag, moved_imag)
    if not keep_imag:
        return (out_real.reshape(leading + (points,)), None)
    out_imag = contract('ka,...kb->...ab', table_imag, moved_real) + contract('ka,...kb->...ab', table_real, moved_imag)
    return (out_real.reshape(leading + (points,)), out_imag.reshape(leading + (points,)))

def pad_zeros(rows):
    return jnp.concatenate([rows, jnp.zeros_like(rows)], axis=-1)

def conj_wide(first_real, first_imag, second_real, second_imag):
    first_real = first_real.astype(jnp.float32)
    first_imag = first_imag.astype(jnp.float32)
    second_real = second_real.astype(jnp.float32)
    second_imag = second_imag.astype(jnp.float32)
    return (first_real * second_real + first_imag * second_imag, first_real * second_imag - first_imag * second_real)

def channel_work(values_rows, cotangent_rows, filter_rows, gain_rows):
    length = values_rows.shape[-1]
    points = 2 * length
    filter_real, filter_imag = forward(pad_zeros(filter_rows), None)
    values_real, values_imag = forward(pad_zeros(values_rows), None)
    cotangent_real, cotangent_imag = forward(pad_zeros(cotangent_rows), None)
    lag_real, lag_imag = conj_wide(filter_real, filter_imag, cotangent_real, cotangent_imag)
    signal = inverse(lag_real.astype(jnp.bfloat16), lag_imag.astype(jnp.bfloat16), False)[0]
    cotangent_wide = cotangent_rows.astype(jnp.float32)
    grad_rows = (signal[..., :length] / points + gain_rows.astype(jnp.float32)[:, None] * cotangent_wide).astype(jnp.bfloat16)
    cross_real, cross_imag = conj_wide(values_real, values_imag, cotangent_real, cotangent_imag)
    cross_real = lax.optimization_barrier(jnp.sum(cross_real, axis=0)).astype(jnp.bfloat16)
    cross_imag = lax.optimization_barrier(jnp.sum(cross_imag, axis=0)).astype(jnp.bfloat16)
    cross_terms = inverse(cross_real, cross_imag, False)[0][..., :length] / points
    gain_terms = lax.optimization_barrier(jnp.sum(cotangent_wide * values_rows.astype(jnp.float32), axis=(0, 2)))
    return (grad_rows, cross_terms, gain_terms)

def reference(values, cotangent, long_filter, bypass):
    block_width = math.gcd(C, 64)
    block_count = C // block_width
    grad_scale = 1.0 / math.sqrt(SEQS * LENGTH)

    def regroup(array):
        return array.reshape(SEQS, LENGTH, block_count, block_width).transpose(2, 0, 3, 1)

    def one_block(operands):
        values_rows, cotangent_rows, filter_rows, gain_rows = operands
        grad_rows, cross_terms, gain_terms = channel_work(values_rows, cotangent_rows, filter_rows, gain_rows)
        return (grad_rows, cross_terms * grad_scale, gain_terms * grad_scale)
    grad_rows, grad_filter, grad_bypass = lax.map(one_block, (regroup(values), regroup(cotangent), long_filter.reshape(block_count, block_width, LENGTH), bypass.reshape(block_count, block_width)))
    grad_values = grad_rows.transpose(1, 3, 0, 2).reshape(SEQS, LENGTH, C)
    return (grad_values, grad_filter.reshape(C, LENGTH), grad_bypass.reshape(C))
```

```python
import functools
import math

import jax
import jax.numpy as jnp
import ml_dtypes
import numpy as np
from jax import lax
from jax.experimental import pallas as pl
from jax.experimental.pallas import tpu as pltpu
from jax.sharding import PartitionSpec as P

MESH = pl.DeviceIdType.MESH
lanes = 128
wide = jnp.float32
narrow = jnp.bfloat16


def tables(sources, points):
    whole = 2 * sources * points
    half = np.arange(sources) + 0.5
    outer = 2.0 * np.pi * np.outer(half, np.arange(sources)) / (2 * sources)
    turn = 2.0 * np.pi * np.outer(half, np.arange(points)) / whole
    inner = 2.0 * np.pi * (np.outer(np.arange(points), np.arange(points)) % points) / points
    cos, sin = np.cos(inner), np.sin(inner)
    as_narrow = lambda table: table.astype(ml_dtypes.bfloat16)
    return (
        as_narrow(np.concatenate([np.cos(outer), -np.sin(outer)], 0)),
        as_narrow(np.block([[cos, -sin], [sin, cos]])),
        as_narrow(np.block([[cos, sin], [-sin, cos]])),
        as_narrow(2.0 / whole * np.concatenate([np.cos(outer).T, -np.sin(outer).T], 1)),
        np.stack([np.cos(turn), np.sin(turn)]).astype(np.float32),
    )


def kernel(
    seqs, copies, scale,
    values_ref, cotangent_ref, filter_ref, gain_ref, outer_ref, inner_ref, back_inner_ref, back_outer_ref, turn_ref,
    grad_ref, grad_filter_ref, grad_gain_ref,
    cot_out, val_out, cot_in, val_in, filters, gains, cot_wide, val_wide, cot_spec, filter_spec,
    grad_out, grad_in, part_out, part_in, gain_out, gain_in, send_sem, recv_sem, near_send_sem, near_recv_sem,
):
    me, mine = lax.axis_index("seq"), lax.axis_index("dp")
    points = values_ref.shape[0]
    group = cot_in.shape[1]
    own = filter_ref.shape[0]
    per_tile = lanes // group

    barrier = pltpu.get_barrier_semaphore()

    def greet(step, carry):
        pl.semaphore_signal(barrier, inc=1, device_id={"seq": lax.rem(me + step, seqs)}, device_id_type=MESH)
        return carry

    lax.fori_loop(1, seqs, greet, 0)
    for step in range(1, copies):
        pl.semaphore_signal(barrier, inc=1, device_id={"dp": lax.rem(mine + step, copies)}, device_id_type=MESH)

    def turn_round(tokens_ref, rows_ref):
        def tile(at, carry):
            block = tokens_ref[:, pl.ds(pl.multiple_of(at * lanes, lanes), lanes)]
            rows_ref[pl.ds(at * per_tile, per_tile)] = block.T.reshape(per_tile, group, points)
            return carry

        lax.fori_loop(0, seqs // per_tile, tile, 0, unroll=2)

    def send(rows_ref, there_ref, which):
        def one(step, carry):
            peer = lax.rem(me + step * 17, seqs)
            pltpu.make_async_remote_copy(
                src_ref=rows_ref.at[peer],
                dst_ref=there_ref.at[me],
                send_sem=send_sem.at[which],
                recv_sem=recv_sem.at[which],
                device_id={"seq": peer},
                device_id_type=MESH,
            ).start()
            return carry

        lax.fori_loop(1, seqs, one, 0)
        there_ref[pl.ds(me, 1)] = rows_ref[pl.ds(me, 1)]

    def all_of(rows_ref, there_ref, which):
        return pltpu.make_async_remote_copy(
            src_ref=rows_ref.at[pl.ds(0, seqs - 1)],
            dst_ref=there_ref.at[pl.ds(0, seqs - 1)],
            send_sem=send_sem.at[which],
            recv_sem=recv_sem.at[which],
            device_id={"seq": lax.rem(me + 1, seqs)},
            device_id_type=MESH,
        )

    def near(which, step, src_ref, dst_ref):
        return pltpu.make_async_remote_copy(
            src_ref=src_ref,
            dst_ref=dst_ref,
            send_sem=near_send_sem.at[which, step],
            recv_sem=near_recv_sem.at[which, step],
            device_id={"dp": lax.rem(mine + step, copies)},
            device_id_type=MESH,
        )

    turn_round(cotangent_ref, cot_out)
    pl.semaphore_wait(barrier, seqs + copies - 2)

    filter_copies = []
    for step in range(1, copies):
        filter_copies.append(near(0, step, filter_ref, filters.at[mine]))
        filter_copies.append(near(1, step, gain_ref, gains.at[mine]))
    for copy in filter_copies:
        copy.start()
    filters[pl.ds(mine, 1)] = filter_ref[...][None]
    gains[pl.ds(mine, 1)] = gain_ref[...][None]
    send(cot_out, cot_in, 0)
    turn_round(values_ref, val_out)
    send(val_out, val_in, 1)

    outer, inner = outer_ref[...], inner_ref[...]
    back_inner, back_outer = back_inner_ref[...], back_outer_ref[...]
    dot = functools.partial(jnp.dot, preferred_element_type=wide)

    def rows_of(wide_ref, channel):
        return wide_ref[pl.ds(channel, seqs, stride=group), :]

    def transform(first, second):
        cos, sin = turn_ref[0], turn_ref[1]
        both = dot(outer, jnp.concatenate([first.astype(narrow), second.astype(narrow)], 1))
        turned = []
        for at in range(2):
            real = both[:seqs, at * points : (at + 1) * points]
            imag = both[seqs:, at * points : (at + 1) * points]
            turned.append(
                jnp.concatenate([(real * cos + imag * sin).astype(narrow), (imag * cos - real * sin).astype(narrow)], 1)
            )
        return [dot(part, inner) for part in turned]

    def times_conj(first, second):
        first_real, first_imag = first[:, :points].astype(wide), first[:, points:].astype(wide)
        second_real, second_imag = second[:, :points].astype(wide), second[:, points:].astype(wide)
        return jnp.concatenate(
            [
                (first_real * second_real + first_imag * second_imag).astype(narrow),
                (first_real * second_imag - first_imag * second_real).astype(narrow),
            ],
            1,
        )

    def invert(first, second):
        cos, sin = turn_ref[0], turn_ref[1]
        turned = []
        for spec in (first, second):
            both = dot(spec, back_inner)
            real, imag = both[:, :points], both[:, points:]
            turned.append(
                jnp.concatenate([(real * cos - imag * sin).astype(narrow), (real * sin + imag * cos).astype(narrow)], 0)
            )
        both = dot(back_outer, jnp.concatenate(turned, 1))
        return both[:, :points], both[:, points:]

    for copy in filter_copies:
        copy.wait_recv()

    def widen_filter(at, carry):
        for copy in range(copies):
            val_wide[pl.ds(at * group + copy * own, own), :] = filters[
                copy, :, pl.ds(pl.multiple_of(at * points, points), points)
            ].astype(wide)
        return carry

    lax.fori_loop(0, seqs, widen_filter, 0, unroll=4)

    def filter_pair(pair, carry):
        at = pair * 2
        specs = transform(rows_of(val_wide, at), rows_of(val_wide, at + 1))
        for offset in range(2):
            filter_spec[at + offset] = specs[offset].astype(narrow)
        return carry

    lax.fori_loop(0, group // 2, filter_pair, 0)

    all_of(cot_out, cot_in, 0).wait_recv()

    def widen_cot(at, carry):
        cot_wide[pl.ds(pl.multiple_of(at * group, group), group), :] = cot_in[at].astype(wide)
        return carry

    lax.fori_loop(0, seqs, widen_cot, 0, unroll=4)

    def grad_pair(pair, carry):
        at = pair * 2
        rows = rows_of(cot_wide, at), rows_of(cot_wide, at + 1)
        specs = transform(*rows)
        lags = []
        for offset in range(2):
            spec = specs[offset].astype(narrow)
            cot_spec[at + offset] = spec
            lags.append(times_conj(filter_spec[at + offset], spec))
        signals = invert(*lags)
        for offset in range(2):
            channel = at + offset
            gain = gains[channel // own, pl.ds(lax.rem(channel, own), 1), :]
            cot_wide[pl.ds(channel, seqs, stride=group), :] = signals[offset] + gain * rows[offset]
        return carry

    lax.fori_loop(0, group // 2, grad_pair, 0)

    def pack_grad(at, carry):
        grad_out[at] = cot_wide[pl.ds(pl.multiple_of(at * group, group), group), :].astype(narrow)
        return carry

    lax.fori_loop(0, seqs, pack_grad, 0, unroll=4)
    send(grad_out, grad_in, 2)

    all_of(val_out, val_in, 1).wait_recv()

    def widen_val(at, total):
        block = val_in[at].astype(wide)
        val_wide[pl.ds(pl.multiple_of(at * group, group), group), :] = block
        return total + block * cot_in[at].astype(wide)

    total = lax.fori_loop(0, seqs, widen_val, jnp.zeros((group, points), wide), unroll=4)
    gain_out[...] = total.reshape(copies, own, points)

    def cross_pair(pair, carry):
        at = pair * 2
        specs = transform(rows_of(val_wide, at), rows_of(val_wide, at + 1))
        parts = [times_conj(specs[offset].astype(narrow), cot_spec[at + offset]) for offset in range(2)]
        signals = invert(*parts)
        for offset in range(2):
            val_wide[pl.ds(at + offset, seqs, stride=group), :] = signals[offset]
        return carry

    lax.fori_loop(0, group // 2, cross_pair, 0)

    def pack_part(at, carry):
        for copy in range(copies):
            part_out[copy, :, pl.ds(pl.multiple_of(at * points, points), points)] = val_wide[
                pl.ds(at * group + copy * own, own), :
            ].astype(narrow)
        return carry

    lax.fori_loop(0, seqs, pack_part, 0, unroll=4)
    part_copies = []
    for step in range(1, copies):
        there = lax.rem(mine + step, copies)
        part_copies.append(near(2, step, part_out.at[there], part_in.at[mine]))
        part_copies.append(near(3, step, gain_out.at[there], gain_in.at[mine]))
    for copy in part_copies:
        copy.start()
    part_in[pl.ds(mine, 1)] = part_out[pl.ds(mine, 1)]
    gain_in[pl.ds(mine, 1)] = gain_out[pl.ds(mine, 1)]

    all_of(grad_out, grad_in, 2).wait_recv()

    def place(at, carry):
        block = grad_in[pl.ds(at * per_tile, per_tile)].reshape(lanes, points)
        grad_ref[:, pl.ds(pl.multiple_of(at * lanes, lanes), lanes)] = block.T
        return carry

    lax.fori_loop(0, seqs // per_tile, place, 0, unroll=2)

    for copy in part_copies:
        copy.wait_recv()

    def sum_parts(at, carry):
        where = pl.ds(pl.multiple_of(at * points, points), points)
        total = part_in[0, :, where].astype(wide)
        for copy in range(1, copies):
            total = total + part_in[copy, :, where].astype(wide)
        grad_filter_ref[:, where] = total * scale
        return carry

    lax.fori_loop(0, seqs, sum_parts, 0, unroll=4)
    total = gain_in[0]
    for copy in range(1, copies):
        total = total + gain_in[copy]
    grad_gain_ref[...] = jnp.broadcast_to(jnp.sum(total, axis=1, keepdims=True) * scale, grad_gain_ref.shape)

    for copy in filter_copies + part_copies:
        copy.wait_send()
    all_of(cot_out, cot_in, 0).wait_send()
    all_of(val_out, val_in, 1).wait_send()
    all_of(grad_out, grad_in, 2).wait_send()


def shards(values, cotangent, long_filter, bypass):
    seqs, copies = lax.axis_size("seq"), lax.axis_size("dp")
    points, channels = values.shape[1:]
    group = channels // seqs
    own, length = long_filter.shape
    scale = 1.0 / math.sqrt(copies * length)
    consts = tables(seqs, points)
    gain = jnp.broadcast_to(bypass.astype(wide)[:, None], (own, lanes))
    vmem = pl.BlockSpec(memory_space=pltpu.VMEM)
    rows = pltpu.VMEM((seqs, group, points), narrow)
    grad, grad_filter, grad_gain = pl.pallas_call(
        functools.partial(kernel, seqs, copies, scale),
        out_shape=(
            jax.ShapeDtypeStruct((points, channels), narrow),
            jax.ShapeDtypeStruct((own, length), wide),
            jax.ShapeDtypeStruct((own, lanes), wide),
        ),
        in_specs=[vmem] * 9,
        out_specs=(vmem,) * 3,
        scratch_shapes=[
            rows,
            rows,
            rows,
            rows,
            pltpu.VMEM((copies, own, length), narrow),
            pltpu.VMEM((copies, own, lanes), wide),
            pltpu.VMEM((seqs * group, points), wide),
            pltpu.VMEM((seqs * group, points), wide),
            pltpu.VMEM((group, seqs, 2 * points), narrow),
            pltpu.VMEM((group, seqs, 2 * points), narrow),
            rows,
            rows,
            pltpu.VMEM((copies, own, length), narrow),
            pltpu.VMEM((copies, own, length), narrow),
            pltpu.VMEM((copies, own, lanes), wide),
            pltpu.VMEM((copies, own, lanes), wide),
            pltpu.SemaphoreType.DMA((3,)),
            pltpu.SemaphoreType.DMA((3,)),
            pltpu.SemaphoreType.DMA((4, copies)),
            pltpu.SemaphoreType.DMA((4, copies)),
        ],
        compiler_params=pltpu.CompilerParams(
            collective_id=0, has_side_effects=True, vmem_limit_bytes=48 * 1024 * 1024
        ),
    )(values[0], cotangent[0], long_filter, gain, *consts)
    return grad[None], grad_filter, grad_gain[:, 0]


def solution(mesh):
    placed = (P("dp", "seq", None), P("dp", "seq", None), P(("seq", "dp"), None), P(("seq", "dp")))
    return jax.shard_map(
        shards,
        mesh=mesh,
        in_specs=placed,
        out_specs=(P("dp", "seq", None), P(("seq", "dp"), None), P(("seq", "dp"))),
        check_vma=False,
    )
```

```python
import functools
import math

import jax
import jax.numpy as jnp
import ml_dtypes
import numpy as np
from jax import lax
from jax.experimental import pallas as pl
from jax.experimental.pallas import tpu as pltpu
from jax.sharding import PartitionSpec as P

MESH = pl.DeviceIdType.MESH
lanes = 128
wide = jnp.float32
narrow = jnp.bfloat16


def tables(sources, points):
    whole = 2 * sources * points
    half = np.arange(sources) + 0.5
    outer = 2.0 * np.pi * np.outer(half, np.arange(sources)) / (2 * sources)
    turn = 2.0 * np.pi * np.outer(half, np.arange(points)) / whole
    inner = 2.0 * np.pi * (np.outer(np.arange(points), np.arange(points)) % points) / points
    cos, sin = np.cos(inner), np.sin(inner)
    as_narrow = lambda table: table.astype(ml_dtypes.bfloat16)
    return (
        as_narrow(np.concatenate([np.cos(outer), -np.sin(outer)], 0)),
        as_narrow(np.block([[cos, -sin], [sin, cos]])),
        as_narrow(np.block([[cos, sin], [-sin, cos]])),
        as_narrow(2.0 / whole * np.concatenate([np.cos(outer).T, -np.sin(outer).T], 1)),
        np.stack([np.cos(turn), np.sin(turn)]).astype(np.float32),
    )


def kernel(
    seqs, copies, cuts, scale,
    values_hbm, cotangent_hbm, filter_hbm, gain_hbm, outer_hbm, inner_hbm, back_inner_hbm, back_outer_hbm, turn_hbm,
    grad_ref, grad_filter_ref, grad_gain_ref,
    values_ref, cotangent_ref, filter_ref, gain_ref, outer_ref, inner_ref, back_inner_ref, back_outer_ref, turn_ref,
    cot_out, val_out, cot_in, val_in, filters, gains, cot_wide, val_wide, cot_spec, filter_spec,
    grad_out, grad_in, part_out, part_in, gain_out, gain_in,
    load_sem, send_sem, recv_sem, near_send_sem, near_recv_sem, ready_sem,
):
    me, mine = lax.axis_index("seq"), lax.axis_index("dp")
    points = values_ref.shape[0]
    group = cot_in.shape[1]
    own = filter_ref.shape[0]
    per_tile = lanes // group
    width = group // cuts
    shares = copies // cuts
    plane = 1 << (seqs.bit_length() // 2)
    columns = seqs // plane

    loads = {}
    for at, (name, src_ref, dst_ref) in enumerate(
        (
            ("cotangent", cotangent_hbm, cotangent_ref),
            ("filter", filter_hbm, filter_ref),
            ("gain", gain_hbm, gain_ref),
            ("values", values_hbm, values_ref),
            ("outer", outer_hbm, outer_ref),
            ("inner", inner_hbm, inner_ref),
            ("turn", turn_hbm, turn_ref),
            ("back_inner", back_inner_hbm, back_inner_ref),
            ("back_outer", back_outer_hbm, back_outer_ref),
        )
    ):
        loads[name] = pltpu.make_async_copy(src_ref, dst_ref, load_sem.at[at])
        loads[name].start()

    barrier = pltpu.get_barrier_semaphore()
    in_plane, in_column = lax.rem(me, plane), me // plane

    def column_peer(step):
        return lax.rem(in_column + step, columns) * plane + in_plane

    def greet_column(step, carry):
        pl.semaphore_signal(barrier, inc=1, device_id={"seq": column_peer(step)}, device_id_type=MESH)
        return carry

    def greet_plane(step, carry):
        peer = in_column * plane + lax.rem(in_plane + step, plane)
        pl.semaphore_signal(barrier, inc=1, device_id={"seq": peer}, device_id_type=MESH)
        return carry

    def tell_column(step, carry):
        pl.semaphore_signal(ready_sem, inc=1, device_id={"seq": column_peer(step)}, device_id_type=MESH)
        return carry

    lax.fori_loop(1, columns, greet_column, 0)
    lax.fori_loop(1, plane, greet_plane, 0)
    for step in range(1, copies):
        pl.semaphore_signal(barrier, inc=1, device_id={"dp": lax.rem(mine + step, copies)}, device_id_type=MESH)

    def turn_round(tokens_ref, rows_ref):
        def tile(at, carry):
            block = tokens_ref[:, pl.ds(pl.multiple_of(at * lanes, lanes), lanes)]
            rows_ref[pl.ds(at * per_tile, per_tile)] = block.T.reshape(per_tile, group, points)
            return carry

        lax.fori_loop(0, seqs // per_tile, tile, 0, unroll=2)

    def send(rows_ref, there_ref, which, cut):
        part = pl.ds(cut * width, width)

        def one(step, carry):
            peer = lax.rem(me + step * 17, seqs)
            pltpu.make_async_remote_copy(
                src_ref=rows_ref.at[peer, part],
                dst_ref=there_ref.at[me, part],
                send_sem=send_sem.at[which, cut],
                recv_sem=recv_sem.at[which, cut],
                device_id={"seq": peer},
                device_id_type=MESH,
            ).start()
            return carry

        lax.fori_loop(1, seqs, one, 0)
        there_ref[pl.ds(me, 1), part] = rows_ref[pl.ds(me, 1), part]

    def all_of(rows_ref, there_ref, which, cut):
        part = pl.ds(cut * width, width)
        return pltpu.make_async_remote_copy(
            src_ref=rows_ref.at[pl.ds(0, seqs - 1), part],
            dst_ref=there_ref.at[pl.ds(0, seqs - 1), part],
            send_sem=send_sem.at[which, cut],
            recv_sem=recv_sem.at[which, cut],
            device_id={"seq": lax.rem(me + 1, seqs)},
            device_id_type=MESH,
        )

    def near(which, step, src_ref, dst_ref):
        return pltpu.make_async_remote_copy(
            src_ref=src_ref,
            dst_ref=dst_ref,
            send_sem=near_send_sem.at[which, step],
            recv_sem=near_recv_sem.at[which, step],
            device_id={"dp": lax.rem(mine + step, copies)},
            device_id_type=MESH,
        )

    pl.semaphore_wait(barrier, plane + columns + copies - 3)
    lax.fori_loop(1, columns, tell_column, 0)
    loads["cotangent"].wait()
    turn_round(cotangent_ref, cot_out)
    loads["filter"].wait()
    loads["gain"].wait()
    filters[pl.ds(mine, 1)] = filter_ref[...][None]
    gains[pl.ds(mine, 1)] = gain_ref[...][None]
    pl.semaphore_wait(ready_sem, columns - 1)

    filter_copies = []
    for step in range(1, copies):
        filter_copies.append(near(0, step, filter_ref, filters.at[mine]))
        filter_copies.append(near(1, step, gain_ref, gains.at[mine]))
    send(cot_out, cot_in, 0, 0)
    for copy in filter_copies:
        copy.start()
    loads["values"].wait()
    turn_round(values_ref, val_out)
    send(val_out, val_in, 1, 0)
    for cut in range(1, cuts):
        send(cot_out, cot_in, 0, cut)
        send(val_out, val_in, 1, cut)

    for name in ("outer", "inner", "turn", "back_inner", "back_outer"):
        loads[name].wait()
    outer, inner = outer_ref[...], inner_ref[...]
    back_inner, back_outer = back_inner_ref[...], back_outer_ref[...]
    dot = functools.partial(jnp.dot, preferred_element_type=wide)

    def rows_of(wide_ref, channel):
        return wide_ref[pl.ds(channel, seqs, stride=group), :]

    def transform(first, second):
        cos, sin = turn_ref[0], turn_ref[1]
        both = dot(outer, jnp.concatenate([first.astype(narrow), second.astype(narrow)], 1))
        turned = []
        for at in range(2):
            real = both[:seqs, at * points : (at + 1) * points]
            imag = both[seqs:, at * points : (at + 1) * points]
            turned.append(
                jnp.concatenate([(real * cos + imag * sin).astype(narrow), (imag * cos - real * sin).astype(narrow)], 1)
            )
        return [dot(part, inner) for part in turned]

    def times_conj(first, second):
        first_real, first_imag = first[:, :points].astype(wide), first[:, points:].astype(wide)
        second_real, second_imag = second[:, :points].astype(wide), second[:, points:].astype(wide)
        return jnp.concatenate(
            [
                (first_real * second_real + first_imag * second_imag).astype(narrow),
                (first_real * second_imag - first_imag * second_real).astype(narrow),
            ],
            1,
        )

    def invert(first, second):
        cos, sin = turn_ref[0], turn_ref[1]
        turned = []
        for spec in (first, second):
            both = dot(spec, back_inner)
            real, imag = both[:, :points], both[:, points:]
            turned.append(
                jnp.concatenate([(real * cos - imag * sin).astype(narrow), (real * sin + imag * cos).astype(narrow)], 0)
            )
        both = dot(back_outer, jnp.concatenate(turned, 1))
        return both[:, :points], both[:, points:]

    for copy in filter_copies:
        copy.wait_recv()

    def widen_filter(at, carry):
        for copy in range(copies):
            val_wide[pl.ds(at * group + copy * own, own), :] = filters[
                copy, :, pl.ds(pl.multiple_of(at * points, points), points)
            ].astype(wide)
        return carry

    lax.fori_loop(0, seqs, widen_filter, 0, unroll=4)

    def filter_pair(pair, carry):
        at = pair * 2
        specs = transform(rows_of(val_wide, at), rows_of(val_wide, at + 1))
        for offset in range(2):
            filter_spec[at + offset] = specs[offset].astype(narrow)
        return carry

    lax.fori_loop(0, group // 2, filter_pair, 0, unroll=2)

    def grad_pair(pair, carry):
        at = pair * 2
        rows = rows_of(cot_wide, at), rows_of(cot_wide, at + 1)
        specs = transform(*rows)
        lags = []
        for offset in range(2):
            spec = specs[offset].astype(narrow)
            cot_spec[at + offset] = spec
            lags.append(times_conj(filter_spec[at + offset], spec))
        signals = invert(*lags)
        for offset in range(2):
            channel = at + offset
            gain = gains[channel // own, pl.ds(lax.rem(channel, own), 1), :]
            cot_wide[pl.ds(channel, seqs, stride=group), :] = signals[offset] + gain * rows[offset]
        return carry

    def cross_pair(pair, carry):
        at = pair * 2
        specs = transform(rows_of(val_wide, at), rows_of(val_wide, at + 1))
        parts = [times_conj(specs[offset].astype(narrow), cot_spec[at + offset]) for offset in range(2)]
        signals = invert(*parts)
        for offset in range(2):
            val_wide[pl.ds(at + offset, seqs, stride=group), :] = signals[offset]
        return carry

    part_copies, gain_copies = [], []
    for step in range(1, copies):
        there = lax.rem(mine + step, copies)
        part_copies.append((there, near(2, step, part_out.at[there], part_in.at[mine])))
        gain_copies.append((there, near(3, step, gain_out.at[there], gain_in.at[mine])))

    for cut in range(cuts):
        part = pl.ds(cut * width, width)

        def rows_at(at):
            return pl.ds(pl.multiple_of(at * group + cut * width, width), width)

        all_of(cot_out, cot_in, 0, cut).wait_recv()

        def widen_cot(at, carry):
            cot_wide[rows_at(at), :] = cot_in[at, part].astype(wide)
            return carry

        lax.fori_loop(0, seqs, widen_cot, 0, unroll=4)
        lax.fori_loop(cut * width // 2, (cut + 1) * width // 2, grad_pair, 0, unroll=2)

        def pack_grad(at, carry):
            grad_out[at, part] = cot_wide[rows_at(at), :].astype(narrow)
            return carry

        lax.fori_loop(0, seqs, pack_grad, 0, unroll=4)
        send(grad_out, grad_in, 2, cut)

        all_of(val_out, val_in, 1, cut).wait_recv()

        def widen_val(at, total):
            block = val_in[at, part].astype(wide)
            val_wide[rows_at(at), :] = block
            return total + block * cot_in[at, part].astype(wide)

        total = lax.fori_loop(0, seqs, widen_val, jnp.zeros((width, points), wide), unroll=4)
        gain_out[pl.ds(cut * shares, shares)] = total.reshape(shares, own, points)
        lax.fori_loop(cut * width // 2, (cut + 1) * width // 2, cross_pair, 0, unroll=2)

        def pack_part(at, carry):
            for copy in range(cut * shares, (cut + 1) * shares):
                part_out[copy, :, pl.ds(pl.multiple_of(at * points, points), points)] = val_wide[
                    pl.ds(at * group + copy * own, own), :
                ].astype(narrow)
            return carry

        lax.fori_loop(0, seqs, pack_part, 0, unroll=4)
        for there, copy in part_copies + gain_copies:
            pl.when(there // shares == cut)(copy.start)

    part_in[pl.ds(mine, 1)] = part_out[pl.ds(mine, 1)]
    gain_in[pl.ds(mine, 1)] = gain_out[pl.ds(mine, 1)]

    def place(at, carry):
        block = grad_in[pl.ds(at * per_tile, per_tile)].reshape(lanes, points)
        grad_ref[:, pl.ds(pl.multiple_of(at * lanes, lanes), lanes)] = block.T
        return carry

    for cut in range(cuts):
        all_of(grad_out, grad_in, 2, cut).wait_recv()
    lax.fori_loop(0, seqs // per_tile, place, 0, unroll=2)

    for there, copy in part_copies + gain_copies:
        copy.wait_recv()

    def sum_parts(at, carry):
        where = pl.ds(pl.multiple_of(at * points, points), points)
        total = part_in[0, :, where].astype(wide)
        for copy in range(1, copies):
            total = total + part_in[copy, :, where].astype(wide)
        grad_filter_ref[:, where] = total * scale
        return carry

    lax.fori_loop(0, seqs, sum_parts, 0, unroll=4)
    total = gain_in[0]
    for copy in range(1, copies):
        total = total + gain_in[copy]
    grad_gain_ref[...] = jnp.broadcast_to(jnp.sum(total, axis=1, keepdims=True) * scale, grad_gain_ref.shape)

    for copy in filter_copies:
        copy.wait_send()
    for there, copy in part_copies + gain_copies:
        copy.wait_send()
    for cut in range(cuts):
        all_of(cot_out, cot_in, 0, cut).wait_send()
        all_of(val_out, val_in, 1, cut).wait_send()
        all_of(grad_out, grad_in, 2, cut).wait_send()


def shards(values, cotangent, long_filter, bypass):
    seqs, copies = lax.axis_size("seq"), lax.axis_size("dp")
    points, channels = values.shape[1:]
    group = channels // seqs
    own, length = long_filter.shape
    scale = 1.0 / math.sqrt(copies * length)
    consts = tables(seqs, points)
    gain = jnp.broadcast_to(bypass.astype(wide)[:, None], (own, lanes))
    vmem, hbm = pl.BlockSpec(memory_space=pltpu.VMEM), pl.BlockSpec(memory_space=pltpu.HBM)
    operands = (values[0], cotangent[0], long_filter, gain, *consts)
    cuts = 2
    rows = pltpu.VMEM((seqs, group, points), narrow)
    grad, grad_filter, grad_gain = pl.pallas_call(
        functools.partial(kernel, seqs, copies, cuts, scale),
        out_shape=(
            jax.ShapeDtypeStruct((points, channels), narrow),
            jax.ShapeDtypeStruct((own, length), wide),
            jax.ShapeDtypeStruct((own, lanes), wide),
        ),
        in_specs=[hbm] * len(operands),
        out_specs=(vmem,) * 3,
        scratch_shapes=[
            *[pltpu.VMEM(operand.shape, operand.dtype) for operand in operands],
            rows,
            rows,
            rows,
            rows,
            pltpu.VMEM((copies, own, length), narrow),
            pltpu.VMEM((copies, own, lanes), wide),
            pltpu.VMEM((seqs * group, points), wide),
            pltpu.VMEM((seqs * group, points), wide),
            pltpu.VMEM((group, seqs, 2 * points), narrow),
            pltpu.VMEM((group, seqs, 2 * points), narrow),
            rows,
            rows,
            pltpu.VMEM((copies, own, length), narrow),
            pltpu.VMEM((copies, own, length), narrow),
            pltpu.VMEM((copies, own, lanes), wide),
            pltpu.VMEM((copies, own, lanes), wide),
            pltpu.SemaphoreType.DMA((len(operands),)),
            pltpu.SemaphoreType.DMA((3, cuts)),
            pltpu.SemaphoreType.DMA((3, cuts)),
            pltpu.SemaphoreType.DMA((4, copies)),
            pltpu.SemaphoreType.DMA((4, copies)),
            pltpu.SemaphoreType.REGULAR,
        ],
        compiler_params=pltpu.CompilerParams(
            collective_id=0, has_side_effects=True, vmem_limit_bytes=48 * 1024 * 1024
        ),
    )(*operands)
    return grad[None], grad_filter, grad_gain[:, 0]


def solution(mesh):
    placed = (P("dp", "seq", None), P("dp", "seq", None), P(("seq", "dp"), None), P(("seq", "dp")))
    return jax.shard_map(
        shards,
        mesh=mesh,
        in_specs=placed,
        out_specs=(P("dp", "seq", None), P(("seq", "dp"), None), P(("seq", "dp"))),
        check_vma=False,
    )
```

```python
import functools
import math

import jax
import jax.numpy as jnp
import ml_dtypes
import numpy as np
from jax import lax
from jax.experimental import pallas as pl
from jax.experimental.pallas import tpu as pltpu
from jax.sharding import PartitionSpec as P

MESH = pl.DeviceIdType.MESH
lanes = 128
wide = jnp.float32
narrow = jnp.bfloat16


def tables(sources, points):
    whole = 2 * sources * points
    half = np.arange(sources) + 0.5
    outer = 2.0 * np.pi * np.outer(half, np.arange(sources)) / (2 * sources)
    turn = 2.0 * np.pi * np.outer(half, np.arange(points)) / whole
    inner = 2.0 * np.pi * (np.outer(np.arange(points), np.arange(points)) % points) / points
    cos, sin = np.cos(inner), np.sin(inner)
    as_narrow = lambda table: table.astype(ml_dtypes.bfloat16)
    return (
        as_narrow(np.concatenate([np.cos(outer), -np.sin(outer)], 0)),
        as_narrow(np.block([[cos, -sin], [sin, cos]])),
        as_narrow(np.block([[cos, sin], [-sin, cos]])),
        as_narrow(2.0 / whole * np.concatenate([np.cos(outer).T, -np.sin(outer).T], 1)),
        np.stack([np.cos(turn), np.sin(turn)]).astype(np.float32),
    )


def kernel(
    seqs, copies, cuts, scale,
    values_hbm, cotangent_hbm, filter_hbm, gain_hbm, outer_hbm, inner_hbm, back_inner_hbm, back_outer_hbm, turn_hbm,
    grad_ref, grad_filter_ref, grad_gain_ref,
    values_ref, cotangent_ref, filter_ref, gain_ref, outer_ref, inner_ref, back_inner_ref, back_outer_ref, turn_ref,
    cot_out, val_out, cot_in, val_in, filters, gains, cot_wide, val_wide, cot_spec, filter_spec,
    grad_out, grad_in, part_out, part_in, passed_in, gain_out, gain_in,
    load_sem, send_sem, recv_sem, near_send_sem, near_recv_sem, ready_sem,
):
    me, mine = lax.axis_index("seq"), lax.axis_index("dp")
    points = values_ref.shape[0]
    group = cot_in.shape[1]
    own = filter_ref.shape[0]
    per_tile = lanes // group
    width = group // cuts
    shares = copies // cuts
    plane = 1 << (seqs.bit_length() // 2)
    columns = seqs // plane
    half = filter_ref.shape[1] // 2
    right, left = 1, copies - 1
    first = 1 - mine // shares

    def rows_of_cut(cut):
        return pl.ds(pl.multiple_of(lax.rem(first + cut, cuts) * width, width), width)

    def dp_at(step):
        return lax.rem(mine + step, copies)

    loads = {}
    for at, (name, src_ref, dst_ref) in enumerate(
        (
            ("cotangent", cotangent_hbm, cotangent_ref),
            ("filter", filter_hbm, filter_ref),
            ("gain", gain_hbm, gain_ref),
            ("values", values_hbm, values_ref),
            ("outer", outer_hbm, outer_ref),
            ("inner", inner_hbm, inner_ref),
            ("turn", turn_hbm, turn_ref),
            ("back_inner", back_inner_hbm, back_inner_ref),
            ("back_outer", back_outer_hbm, back_outer_ref),
        )
    ):
        loads[name] = pltpu.make_async_copy(src_ref, dst_ref, load_sem.at[at])
        loads[name].start()

    barrier = pltpu.get_barrier_semaphore()
    in_plane, in_column = lax.rem(me, plane), me // plane

    def column_peer(step):
        return lax.rem(in_column + step, columns) * plane + in_plane

    def greet_column(step, carry):
        pl.semaphore_signal(barrier, inc=1, device_id={"seq": column_peer(step)}, device_id_type=MESH)
        return carry

    def greet_plane(step, carry):
        peer = in_column * plane + lax.rem(in_plane + step, plane)
        pl.semaphore_signal(barrier, inc=1, device_id={"seq": peer}, device_id_type=MESH)
        return carry

    def tell_column(step, carry):
        pl.semaphore_signal(ready_sem, inc=1, device_id={"seq": column_peer(step)}, device_id_type=MESH)
        return carry

    lax.fori_loop(1, columns, greet_column, 0)
    lax.fori_loop(1, plane, greet_plane, 0)
    for step in range(1, copies):
        pl.semaphore_signal(barrier, inc=1, device_id={"dp": lax.rem(mine + step, copies)}, device_id_type=MESH)

    def turn_round(tokens_ref, rows_ref):
        def tile(at, carry):
            block = tokens_ref[:, pl.ds(pl.multiple_of(at * lanes, lanes), lanes)]
            rows_ref[pl.ds(at * per_tile, per_tile)] = block.T.reshape(per_tile, group, points)
            return carry

        lax.fori_loop(0, seqs // per_tile, tile, 0, unroll=2)

    def send(rows_ref, there_ref, which, cut):
        part = rows_of_cut(cut)

        def one(step, carry):
            peer = lax.rem(me + step * 17, seqs)
            pltpu.make_async_remote_copy(
                src_ref=rows_ref.at[peer, part],
                dst_ref=there_ref.at[me, part],
                send_sem=send_sem.at[which, cut],
                recv_sem=recv_sem.at[which, cut],
                device_id={"seq": peer},
                device_id_type=MESH,
            ).start()
            return carry

        lax.fori_loop(1, seqs, one, 0)
        there_ref[pl.ds(me, 1), part] = rows_ref[pl.ds(me, 1), part]

    def all_of(rows_ref, there_ref, which, cut):
        part = rows_of_cut(cut)
        return pltpu.make_async_remote_copy(
            src_ref=rows_ref.at[pl.ds(0, seqs - 1), part],
            dst_ref=there_ref.at[pl.ds(0, seqs - 1), part],
            send_sem=send_sem.at[which, cut],
            recv_sem=recv_sem.at[which, cut],
            device_id={"seq": lax.rem(me + 1, seqs)},
            device_id_type=MESH,
        )

    def near(which, step, src_ref, dst_ref):
        return pltpu.make_async_remote_copy(
            src_ref=src_ref,
            dst_ref=dst_ref,
            send_sem=near_send_sem.at[which, step],
            recv_sem=near_recv_sem.at[which, step],
            device_id={"dp": lax.rem(mine + step, copies)},
            device_id_type=MESH,
        )

    pl.semaphore_wait(barrier, plane + columns + copies - 3)
    lax.fori_loop(1, columns, tell_column, 0)
    loads["cotangent"].wait()
    turn_round(cotangent_ref, cot_out)
    loads["filter"].wait()
    loads["gain"].wait()
    filters[pl.ds(mine, 1)] = filter_ref[...][None]
    gains[pl.ds(mine, 1)] = gain_ref[...][None]
    pl.semaphore_wait(ready_sem, columns - 1)

    filter_copies = [near(0, step, filter_ref, filters.at[mine]) for step in (right, left)]
    gain_copies = [near(1, step, gain_ref, gains.at[mine]) for step in range(1, copies)]
    filter_passes = []
    for step, start in ((right, 0), (left, half)):
        passed = filters.at[dp_at(copies - step), :, pl.ds(start, half)]
        filter_passes.append(near(4, step, passed, passed))
    send(cot_out, cot_in, 0, 0)
    for copy in filter_copies + gain_copies:
        copy.start()
    loads["values"].wait()
    turn_round(values_ref, val_out)
    send(val_out, val_in, 1, 0)
    for copy, onward in zip(filter_copies, filter_passes):
        copy.wait_recv()
        onward.start()
    for cut in range(1, cuts):
        send(cot_out, cot_in, 0, cut)
        send(val_out, val_in, 1, cut)

    for name in ("outer", "inner", "turn", "back_inner", "back_outer"):
        loads[name].wait()
    outer, inner = outer_ref[...], inner_ref[...]
    back_inner, back_outer = back_inner_ref[...], back_outer_ref[...]
    dot = functools.partial(jnp.dot, preferred_element_type=wide)

    def rows_of(wide_ref, channel):
        return wide_ref[pl.ds(channel, seqs, stride=group), :]

    def transform(first, second):
        cos, sin = turn_ref[0], turn_ref[1]
        both = dot(outer, jnp.concatenate([first.astype(narrow), second.astype(narrow)], 1))
        turned = []
        for at in range(2):
            real = both[:seqs, at * points : (at + 1) * points]
            imag = both[seqs:, at * points : (at + 1) * points]
            turned.append(
                jnp.concatenate([(real * cos + imag * sin).astype(narrow), (imag * cos - real * sin).astype(narrow)], 1)
            )
        return [dot(part, inner) for part in turned]

    def times_conj(first, second):
        first_real, first_imag = first[:, :points].astype(wide), first[:, points:].astype(wide)
        second_real, second_imag = second[:, :points].astype(wide), second[:, points:].astype(wide)
        return jnp.concatenate(
            [
                (first_real * second_real + first_imag * second_imag).astype(narrow),
                (first_real * second_imag - first_imag * second_real).astype(narrow),
            ],
            1,
        )

    def invert(first, second):
        cos, sin = turn_ref[0], turn_ref[1]
        turned = []
        for spec in (first, second):
            both = dot(spec, back_inner)
            real, imag = both[:, :points], both[:, points:]
            turned.append(
                jnp.concatenate([(real * cos - imag * sin).astype(narrow), (real * sin + imag * cos).astype(narrow)], 0)
            )
        both = dot(back_outer, jnp.concatenate(turned, 1))
        return both[:, :points], both[:, points:]

    for copy in filter_passes + gain_copies:
        copy.wait_recv()

    def widen_filter(at, carry):
        for copy in range(copies):
            val_wide[pl.ds(at * group + copy * own, own), :] = filters[
                copy, :, pl.ds(pl.multiple_of(at * points, points), points)
            ].astype(wide)
        return carry

    lax.fori_loop(0, seqs, widen_filter, 0, unroll=4)

    def filter_pair(pair, carry):
        at = pair * 2
        specs = transform(rows_of(val_wide, at), rows_of(val_wide, at + 1))
        for offset in range(2):
            filter_spec[at + offset] = specs[offset].astype(narrow)
        return carry

    lax.fori_loop(0, group // 2, filter_pair, 0, unroll=2)

    def grad_pair(pair, carry):
        at = pair * 2
        rows = rows_of(cot_wide, at), rows_of(cot_wide, at + 1)
        specs = transform(*rows)
        lags = []
        for offset in range(2):
            spec = specs[offset].astype(narrow)
            cot_spec[at + offset] = spec
            lags.append(times_conj(filter_spec[at + offset], spec))
        signals = invert(*lags)
        for offset in range(2):
            channel = at + offset
            gain = gains[channel // own, pl.ds(lax.rem(channel, own), 1), :]
            cot_wide[pl.ds(channel, seqs, stride=group), :] = signals[offset] + gain * rows[offset]
        return carry

    def cross_pair(pair, carry):
        at = pair * 2
        specs = transform(rows_of(val_wide, at), rows_of(val_wide, at + 1))
        parts = [times_conj(specs[offset].astype(narrow), cot_spec[at + offset]) for offset in range(2)]
        signals = invert(*parts)
        for offset in range(2):
            val_wide[pl.ds(at + offset, seqs, stride=group), :] = signals[offset]
        return carry

    part_copies = {}
    pass_copies = []
    for step, start in ((right, 0), (left, half)):
        side = 0 if step == right else 1
        part_copies[step] = near(2, step, part_out.at[dp_at(step)], part_in.at[side])
        pass_copies.append(near(5, step, part_out.at[dp_at(2), :, pl.ds(start, half)], passed_in.at[side]))
    gain_sums = [near(3, step, gain_out.at[dp_at(step)], gain_in.at[mine]) for step in range(1, copies)]

    def hand_over(step):
        side = 0 if step == right else 1
        there = dp_at(step)
        pass_copies[side].wait_recv()

        def add(at, carry):
            here = pl.multiple_of(at * points, points)
            where = pl.ds(side * half + here, points)
            sent_on = part_out[there, :, where].astype(wide) + passed_in[side, :, pl.ds(here, points)].astype(wide)
            part_out[there, :, where] = sent_on.astype(narrow)
            return carry

        lax.fori_loop(0, seqs // 2, add, 0, unroll=min(4, seqs // 2))
        part_copies[step].start()

    even = lax.rem(mine, 2) == 0

    for cut in range(cuts):
        part = rows_of_cut(cut)
        begin = lax.rem(first + cut, cuts)

        def rows_at(at):
            return pl.ds(pl.multiple_of(at * group + begin * width, width), width)

        all_of(cot_out, cot_in, 0, cut).wait_recv()

        def widen_cot(at, carry):
            cot_wide[rows_at(at), :] = cot_in[at, part].astype(wide)
            return carry

        lax.fori_loop(0, seqs, widen_cot, 0, unroll=4)
        lax.fori_loop(0, width // 2, lambda pair, carry: grad_pair(begin * (width // 2) + pair, carry), 0, unroll=2)

        def pack_grad(at, carry):
            grad_out[at, part] = cot_wide[rows_at(at), :].astype(narrow)
            return carry

        lax.fori_loop(0, seqs, pack_grad, 0, unroll=4)
        send(grad_out, grad_in, 2, cut)

        if cut == 1:
            pl.when(even)(lambda: hand_over(left))
            pl.when(jnp.logical_not(even))(lambda: hand_over(right))
        all_of(val_out, val_in, 1, cut).wait_recv()

        def widen_val(at, total):
            block = val_in[at, part].astype(wide)
            val_wide[rows_at(at), :] = block
            return total + block * cot_in[at, part].astype(wide)

        total = lax.fori_loop(0, seqs, widen_val, jnp.zeros((width, points), wide), unroll=4)
        gain_out[pl.ds(begin * shares, shares)] = total.reshape(shares, own, points)
        lax.fori_loop(0, width // 2, lambda pair, carry: cross_pair(begin * (width // 2) + pair, carry), 0, unroll=2)

        def pack_part(at, carry):
            for share in range(shares):
                copy = begin * shares + share
                part_out[copy, :, pl.ds(pl.multiple_of(at * points, points), points)] = val_wide[
                    pl.ds(pl.multiple_of(at * group + copy * own, own), own), :
                ].astype(narrow)
            return carry

        lax.fori_loop(0, seqs, pack_part, 0, unroll=4)
        if cut == 0:
            for copy in pass_copies:
                copy.start()
        else:
            pl.when(even)(lambda: hand_over(right))
            pl.when(jnp.logical_not(even))(lambda: hand_over(left))
    for copy in gain_sums:
        copy.start()
    gain_in[pl.ds(mine, 1)] = gain_out[pl.ds(mine, 1)]

    def place(at, carry):
        block = grad_in[pl.ds(at * per_tile, per_tile)].reshape(lanes, points)
        grad_ref[:, pl.ds(pl.multiple_of(at * lanes, lanes), lanes)] = block.T
        return carry

    for cut in range(cuts):
        all_of(grad_out, grad_in, 2, cut).wait_recv()
    lax.fori_loop(0, seqs // per_tile, place, 0, unroll=2)

    for copy in [*part_copies.values(), *gain_sums]:
        copy.wait_recv()

    def sum_parts(at, carry):
        where = pl.ds(pl.multiple_of(at * points, points), points)
        total = part_out[mine, :, where].astype(wide) + part_in[0, :, where].astype(wide)
        grad_filter_ref[:, where] = (total + part_in[1, :, where].astype(wide)) * scale
        return carry

    lax.fori_loop(0, seqs, sum_parts, 0, unroll=4)
    total = gain_in[0]
    for copy in range(1, copies):
        total = total + gain_in[copy]
    grad_gain_ref[...] = jnp.broadcast_to(jnp.sum(total, axis=1, keepdims=True) * scale, grad_gain_ref.shape)

    for copy in filter_copies + gain_copies + filter_passes + pass_copies + [*part_copies.values(), *gain_sums]:
        copy.wait_send()
    for cut in range(cuts):
        all_of(cot_out, cot_in, 0, cut).wait_send()
        all_of(val_out, val_in, 1, cut).wait_send()
        all_of(grad_out, grad_in, 2, cut).wait_send()


def shards(values, cotangent, long_filter, bypass):
    seqs, copies = lax.axis_size("seq"), lax.axis_size("dp")
    points, channels = values.shape[1:]
    group = channels // seqs
    own, length = long_filter.shape
    scale = 1.0 / math.sqrt(copies * length)
    consts = tables(seqs, points)
    gain = jnp.broadcast_to(bypass.astype(wide)[:, None], (own, lanes))
    vmem, hbm = pl.BlockSpec(memory_space=pltpu.VMEM), pl.BlockSpec(memory_space=pltpu.HBM)
    operands = (values[0], cotangent[0], long_filter, gain, *consts)
    cuts = 2
    rows = pltpu.VMEM((seqs, group, points), narrow)
    grad, grad_filter, grad_gain = pl.pallas_call(
        functools.partial(kernel, seqs, copies, cuts, scale),
        out_shape=(
            jax.ShapeDtypeStruct((points, channels), narrow),
            jax.ShapeDtypeStruct((own, length), wide),
            jax.ShapeDtypeStruct((own, lanes), wide),
        ),
        in_specs=[hbm] * len(operands),
        out_specs=(vmem,) * 3,
        scratch_shapes=[
            *[pltpu.VMEM(operand.shape, operand.dtype) for operand in operands],
            rows,
            rows,
            rows,
            rows,
            pltpu.VMEM((copies, own, length), narrow),
            pltpu.VMEM((copies, own, lanes), wide),
            pltpu.VMEM((seqs * group, points), wide),
            pltpu.VMEM((seqs * group, points), wide),
            pltpu.VMEM((group, seqs, 2 * points), narrow),
            pltpu.VMEM((group, seqs, 2 * points), narrow),
            rows,
            rows,
            pltpu.VMEM((copies, own, length), narrow),
            pltpu.VMEM((2, own, length), narrow),
            pltpu.VMEM((2, own, length // 2), narrow),
            pltpu.VMEM((copies, own, lanes), wide),
            pltpu.VMEM((copies, own, lanes), wide),
            pltpu.SemaphoreType.DMA((len(operands),)),
            pltpu.SemaphoreType.DMA((3, cuts)),
            pltpu.SemaphoreType.DMA((3, cuts)),
            pltpu.SemaphoreType.DMA((6, copies)),
            pltpu.SemaphoreType.DMA((6, copies)),
            pltpu.SemaphoreType.REGULAR,
        ],
        compiler_params=pltpu.CompilerParams(
            collective_id=0, has_side_effects=True, vmem_limit_bytes=64 * 1024 * 1024
        ),
    )(*operands)
    return grad[None], grad_filter, grad_gain[:, 0]


def solution(mesh):
    placed = (P("dp", "seq", None), P("dp", "seq", None), P(("seq", "dp"), None), P(("seq", "dp")))
    return jax.shard_map(
        shards,
        mesh=mesh,
        in_specs=placed,
        out_specs=(P("dp", "seq", None), P(("seq", "dp"), None), P(("seq", "dp"))),
        check_vma=False,
    )
```

```python
import functools
import math

import jax
import jax.numpy as jnp
import ml_dtypes
import numpy as np
from jax import lax
from jax.experimental import pallas as pl
from jax.experimental.pallas import tpu as pltpu
from jax.sharding import PartitionSpec as P

MESH = pl.DeviceIdType.MESH
lanes = 128
wide = jnp.float32
unroll = 4
narrow = jnp.bfloat16


def tables(sources, points):
    whole = 2 * sources * points
    half = np.arange(sources) + 0.5
    outer = 2.0 * np.pi * np.outer(half, np.arange(sources)) / (2 * sources)
    turn = 2.0 * np.pi * np.outer(half, np.arange(points)) / whole
    inner = 2.0 * np.pi * (np.outer(np.arange(points), np.arange(points)) % points) / points
    cos, sin = np.cos(inner), np.sin(inner)
    as_narrow = lambda table: table.astype(ml_dtypes.bfloat16)
    return (
        as_narrow(np.concatenate([np.cos(outer), -np.sin(outer)], 0)),
        as_narrow(np.block([[cos, -sin], [sin, cos]])),
        as_narrow(np.block([[cos, sin], [-sin, cos]])),
        as_narrow(2.0 / whole * np.concatenate([np.cos(outer).T, -np.sin(outer).T], 1)),
        np.stack([np.cos(turn), np.sin(turn)]).astype(np.float32),
    )


def kernel(
    seqs, copies, cuts, scale,
    values_hbm, cotangent_hbm, filter_hbm, gain_hbm, outer_hbm, inner_hbm, back_inner_hbm, back_outer_hbm, turn_hbm,
    grad_ref, grad_filter_ref, grad_gain_ref,
    values_ref, cotangent_ref, filter_ref, gain_ref, outer_ref, inner_ref, back_inner_ref, back_outer_ref, turn_ref,
    cot_out, val_out, cot_in, val_in, filters, gains, cot_wide, val_wide, cot_spec, filter_spec,
    grad_out, grad_in, part_out, part_in, passed_in, gain_out, gain_in,
    load_sem, send_sem, recv_sem, near_send_sem, near_recv_sem, ready_sem,
):
    me, mine = lax.axis_index("seq"), lax.axis_index("dp")
    points = values_ref.shape[0]
    group = cot_in.shape[1]
    own = filter_ref.shape[0]
    per_tile = lanes // group
    width = group // cuts
    shares = copies // cuts
    plane = 1 << (seqs.bit_length() // 2)
    columns = seqs // plane
    half = filter_ref.shape[1] // 2
    right, left = 1, copies - 1
    first = 1 - mine // shares

    def rows_of_cut(cut):
        return pl.ds(pl.multiple_of(lax.rem(first + cut, cuts) * width, width), width)

    def dp_at(step):
        return lax.rem(mine + step, copies)

    loads = {}
    for at, (name, src_ref, dst_ref) in enumerate(
        (
            ("cotangent", cotangent_hbm, cotangent_ref),
            ("filter", filter_hbm, filter_ref),
            ("gain", gain_hbm, gain_ref),
            ("values", values_hbm, values_ref),
            ("outer", outer_hbm, outer_ref),
            ("inner", inner_hbm, inner_ref),
            ("turn", turn_hbm, turn_ref),
            ("back_inner", back_inner_hbm, back_inner_ref),
            ("back_outer", back_outer_hbm, back_outer_ref),
        )
    ):
        loads[name] = pltpu.make_async_copy(src_ref, dst_ref, load_sem.at[at])
        loads[name].start()

    barrier = pltpu.get_barrier_semaphore()
    in_plane, in_column = lax.rem(me, plane), me // plane

    def column_peer(step):
        return lax.rem(in_column + step, columns) * plane + in_plane

    def greet_column(step, carry):
        pl.semaphore_signal(barrier, inc=1, device_id={"seq": column_peer(step)}, device_id_type=MESH)
        return carry

    def greet_plane(step, carry):
        peer = in_column * plane + lax.rem(in_plane + step, plane)
        pl.semaphore_signal(barrier, inc=1, device_id={"seq": peer}, device_id_type=MESH)
        return carry

    def tell_column(step, carry):
        pl.semaphore_signal(ready_sem, inc=1, device_id={"seq": column_peer(step)}, device_id_type=MESH)
        return carry

    lax.fori_loop(1, columns, greet_column, 0)
    lax.fori_loop(1, plane, greet_plane, 0)
    for step in range(1, copies):
        pl.semaphore_signal(barrier, inc=1, device_id={"dp": lax.rem(mine + step, copies)}, device_id_type=MESH)

    def turn_round(tokens_ref, rows_ref):
        def tile(at, carry):
            block = tokens_ref[:, pl.ds(pl.multiple_of(at * lanes, lanes), lanes)]
            rows_ref[pl.ds(at * per_tile, per_tile)] = block.T.reshape(per_tile, group, points)
            return carry

        lax.fori_loop(0, seqs // per_tile, tile, 0, unroll=2)

    def send(rows_ref, there_ref, which, cut):
        part = rows_of_cut(cut)

        def one(step, carry):
            peer = lax.rem(me + step * 17, seqs)
            pltpu.make_async_remote_copy(
                src_ref=rows_ref.at[peer, part],
                dst_ref=there_ref.at[me, part],
                send_sem=send_sem.at[which, cut],
                recv_sem=recv_sem.at[which, cut],
                device_id={"seq": peer},
                device_id_type=MESH,
            ).start()
            return carry

        lax.fori_loop(1, seqs, one, 0)
        there_ref[pl.ds(me, 1), part] = rows_ref[pl.ds(me, 1), part]

    def all_of(rows_ref, there_ref, which, cut):
        part = rows_of_cut(cut)
        return pltpu.make_async_remote_copy(
            src_ref=rows_ref.at[pl.ds(0, seqs - 1), part],
            dst_ref=there_ref.at[pl.ds(0, seqs - 1), part],
            send_sem=send_sem.at[which, cut],
            recv_sem=recv_sem.at[which, cut],
            device_id={"seq": lax.rem(me + 1, seqs)},
            device_id_type=MESH,
        )

    def near(which, step, src_ref, dst_ref):
        return pltpu.make_async_remote_copy(
            src_ref=src_ref,
            dst_ref=dst_ref,
            send_sem=near_send_sem.at[which, step],
            recv_sem=near_recv_sem.at[which, step],
            device_id={"dp": lax.rem(mine + step, copies)},
            device_id_type=MESH,
        )

    pl.semaphore_wait(barrier, plane + columns + copies - 3)
    lax.fori_loop(1, columns, tell_column, 0)
    loads["cotangent"].wait()
    turn_round(cotangent_ref, cot_out)
    loads["filter"].wait()
    loads["gain"].wait()
    filters[pl.ds(mine, 1)] = filter_ref[...][None]
    diagonal = lax.broadcasted_iota(jnp.int32, (own, own), 0) == lax.broadcasted_iota(jnp.int32, (own, own), 1)
    gain_square = jnp.where(diagonal, jnp.broadcast_to(gain_ref[...].astype(wide), (own, own)), 0.0)
    gains[pl.ds(mine, 1)] = jnp.broadcast_to(jnp.sum(gain_square, axis=1, keepdims=True), (own, lanes))[None]
    pl.semaphore_wait(ready_sem, columns - 1)

    filter_copies = [near(0, step, filter_ref, filters.at[mine]) for step in (right, left)]
    gain_copies = [near(1, step, gains.at[mine], gains.at[mine]) for step in range(1, copies)]
    filter_passes = []
    for step, start in ((right, 0), (left, half)):
        passed = filters.at[dp_at(copies - step), :, pl.ds(start, half)]
        filter_passes.append(near(4, step, passed, passed))
    send(cot_out, cot_in, 0, 0)
    for copy in filter_copies + gain_copies:
        copy.start()
    loads["values"].wait()
    turn_round(values_ref, val_out)
    send(val_out, val_in, 1, 0)
    for copy, onward in zip(filter_copies, filter_passes):
        copy.wait_recv()
        onward.start()
    for cut in range(1, cuts):
        send(cot_out, cot_in, 0, cut)
        send(val_out, val_in, 1, cut)

    for name in ("outer", "inner", "turn", "back_inner", "back_outer"):
        loads[name].wait()
    outer, inner = outer_ref[...], inner_ref[...]
    back_inner, back_outer = back_inner_ref[...], back_outer_ref[...]
    dot = functools.partial(jnp.dot, preferred_element_type=wide)

    def rows_of(wide_ref, channel):
        return wide_ref[pl.ds(channel, seqs, stride=group), :]

    def transform(first, second):
        cos, sin = turn_ref[0], turn_ref[1]
        both = dot(outer, jnp.concatenate([first.astype(narrow), second.astype(narrow)], 1))
        turned = []
        for at in range(2):
            real = both[:seqs, at * points : (at + 1) * points]
            imag = both[seqs:, at * points : (at + 1) * points]
            turned.append(
                jnp.concatenate([(real * cos + imag * sin).astype(narrow), (imag * cos - real * sin).astype(narrow)], 1)
            )
        return [dot(part, inner) for part in turned]

    def times_conj(first, second):
        first_real, first_imag = first[:, :points].astype(wide), first[:, points:].astype(wide)
        second_real, second_imag = second[:, :points].astype(wide), second[:, points:].astype(wide)
        return jnp.concatenate(
            [
                (first_real * second_real + first_imag * second_imag).astype(narrow),
                (first_real * second_imag - first_imag * second_real).astype(narrow),
            ],
            1,
        )

    def invert(first, second):
        cos, sin = turn_ref[0], turn_ref[1]
        turned = []
        for spec in (first, second):
            both = dot(spec, back_inner)
            real, imag = both[:, :points], both[:, points:]
            turned.append(
                jnp.concatenate([(real * cos - imag * sin).astype(narrow), (real * sin + imag * cos).astype(narrow)], 0)
            )
        both = dot(back_outer, jnp.concatenate(turned, 1))
        return both[:, :points], both[:, points:]

    for copy in filter_passes + gain_copies:
        copy.wait_recv()

    def widen_filter(at, carry):
        for copy in range(copies):
            val_wide[pl.ds(at * group + copy * own, own), :] = filters[
                copy, :, pl.ds(pl.multiple_of(at * points, points), points)
            ].astype(wide)
        return carry

    lax.fori_loop(0, seqs, widen_filter, 0, unroll=4)

    def filter_pair(pair, carry):
        at = pair * 2
        specs = transform(rows_of(val_wide, at), rows_of(val_wide, at + 1))
        for offset in range(2):
            filter_spec[at + offset] = specs[offset].astype(narrow)
        return carry

    lax.fori_loop(0, group // 2, filter_pair, 0, unroll=unroll)

    def grad_pair(pair, carry):
        at = pair * 2
        rows = rows_of(cot_wide, at), rows_of(cot_wide, at + 1)
        specs = transform(*rows)
        lags = []
        for offset in range(2):
            spec = specs[offset].astype(narrow)
            cot_spec[at + offset] = spec
            lags.append(times_conj(filter_spec[at + offset], spec))
        signals = invert(*lags)
        for offset in range(2):
            channel = at + offset
            gain = gains[channel // own, pl.ds(lax.rem(channel, own), 1), :]
            cot_wide[pl.ds(channel, seqs, stride=group), :] = signals[offset] + gain * rows[offset]
        return carry

    def cross_pair(pair, carry):
        at = pair * 2
        specs = transform(rows_of(val_wide, at), rows_of(val_wide, at + 1))
        parts = [times_conj(specs[offset].astype(narrow), cot_spec[at + offset]) for offset in range(2)]
        signals = invert(*parts)
        for offset in range(2):
            val_wide[pl.ds(at + offset, seqs, stride=group), :] = signals[offset]
        return carry

    part_copies = {}
    pass_copies = []
    for step, start in ((right, 0), (left, half)):
        side = 0 if step == right else 1
        part_copies[step] = near(2, step, part_out.at[dp_at(step)], part_in.at[side])
        pass_copies.append(near(5, step, part_out.at[dp_at(2), :, pl.ds(start, half)], passed_in.at[side]))
    gain_sums = [near(3, step, gain_out.at[dp_at(step)], gain_in.at[mine]) for step in range(1, copies)]

    def hand_over(step):
        side = 0 if step == right else 1
        there = dp_at(step)
        pass_copies[side].wait_recv()

        def add(at, carry):
            here = pl.multiple_of(at * points, points)
            where = pl.ds(side * half + here, points)
            sent_on = part_out[there, :, where].astype(wide) + passed_in[side, :, pl.ds(here, points)].astype(wide)
            part_out[there, :, where] = sent_on.astype(narrow)
            return carry

        lax.fori_loop(0, seqs // 2, add, 0, unroll=min(4, seqs // 2))
        part_copies[step].start()

    even = lax.rem(mine, 2) == 0

    for cut in range(cuts):
        part = rows_of_cut(cut)
        begin = lax.rem(first + cut, cuts)

        def rows_at(at):
            return pl.ds(pl.multiple_of(at * group + begin * width, width), width)

        all_of(cot_out, cot_in, 0, cut).wait_recv()

        def widen_cot(at, carry):
            cot_wide[rows_at(at), :] = cot_in[at, part].astype(wide)
            return carry

        lax.fori_loop(0, seqs, widen_cot, 0, unroll=4)
        lax.fori_loop(0, width // 2, lambda pair, carry: grad_pair(begin * (width // 2) + pair, carry), 0, unroll=unroll)

        def pack_grad(at, carry):
            grad_out[at, part] = cot_wide[rows_at(at), :].astype(narrow)
            return carry

        lax.fori_loop(0, seqs, pack_grad, 0, unroll=4)
        send(grad_out, grad_in, 2, cut)

        if cut == 1:
            pl.when(even)(lambda: hand_over(left))
            pl.when(jnp.logical_not(even))(lambda: hand_over(right))
        all_of(val_out, val_in, 1, cut).wait_recv()

        def widen_val(at, total):
            block = val_in[at, part].astype(wide)
            val_wide[rows_at(at), :] = block
            return total + block * cot_in[at, part].astype(wide)

        total = lax.fori_loop(0, seqs, widen_val, jnp.zeros((width, points), wide), unroll=4)
        gain_out[pl.ds(begin * shares, shares)] = total.reshape(shares, own, points)
        lax.fori_loop(0, width // 2, lambda pair, carry: cross_pair(begin * (width // 2) + pair, carry), 0, unroll=unroll)

        def pack_part(at, carry):
            for share in range(shares):
                copy = begin * shares + share
                part_out[copy, :, pl.ds(pl.multiple_of(at * points, points), points)] = val_wide[
                    pl.ds(pl.multiple_of(at * group + copy * own, own), own), :
                ].astype(narrow)
            return carry

        lax.fori_loop(0, seqs, pack_part, 0, unroll=4)
        if cut == 0:
            for copy in pass_copies:
                copy.start()
        else:
            pl.when(even)(lambda: hand_over(right))
            pl.when(jnp.logical_not(even))(lambda: hand_over(left))
    for copy in gain_sums:
        copy.start()
    gain_in[pl.ds(mine, 1)] = gain_out[pl.ds(mine, 1)]

    def place(at, carry):
        block = grad_in[pl.ds(at * per_tile, per_tile)].reshape(lanes, points)
        grad_ref[:, pl.ds(pl.multiple_of(at * lanes, lanes), lanes)] = block.T
        return carry

    for cut in range(cuts):
        all_of(grad_out, grad_in, 2, cut).wait_recv()
    lax.fori_loop(0, seqs // per_tile, place, 0, unroll=2)

    for copy in [*part_copies.values(), *gain_sums]:
        copy.wait_recv()

    def sum_parts(at, carry):
        where = pl.ds(pl.multiple_of(at * points, points), points)
        total = part_out[mine, :, where].astype(wide) + part_in[0, :, where].astype(wide)
        grad_filter_ref[:, where] = (total + part_in[1, :, where].astype(wide)) * scale
        return carry

    lax.fori_loop(0, seqs, sum_parts, 0, unroll=4)
    total = gain_in[0]
    for copy in range(1, copies):
        total = total + gain_in[copy]
    total = jnp.broadcast_to(jnp.sum(total, axis=1, keepdims=True) * scale, (own, own))
    grad_gain_ref[...] = jnp.sum(jnp.where(diagonal, total, 0.0), axis=0, keepdims=True)

    for copy in filter_copies + gain_copies + filter_passes + pass_copies + [*part_copies.values(), *gain_sums]:
        copy.wait_send()
    for cut in range(cuts):
        all_of(cot_out, cot_in, 0, cut).wait_send()
        all_of(val_out, val_in, 1, cut).wait_send()
        all_of(grad_out, grad_in, 2, cut).wait_send()


def shards(values, cotangent, long_filter, bypass):
    seqs, copies = lax.axis_size("seq"), lax.axis_size("dp")
    points, channels = values.shape[1:]
    group = channels // seqs
    own, length = long_filter.shape
    scale = 1.0 / math.sqrt(copies * length)
    consts = tables(seqs, points)
    vmem, hbm = pl.BlockSpec(memory_space=pltpu.VMEM), pl.BlockSpec(memory_space=pltpu.HBM)
    operands = (values[0], cotangent[0], long_filter, bypass[None], *consts)
    operands = [pltpu.with_memory_space_constraint(operand, pltpu.HBM) for operand in operands]
    cuts = 2
    rows = pltpu.VMEM((seqs, group, points), narrow)
    grad, grad_filter, grad_gain = pl.pallas_call(
        functools.partial(kernel, seqs, copies, cuts, scale),
        out_shape=(
            pltpu.VMEM((points, channels), narrow),
            pltpu.VMEM((own, length), wide),
            pltpu.VMEM((1, own), wide),
        ),
        in_specs=[hbm] * len(operands),
        out_specs=(vmem,) * 3,
        scratch_shapes=[
            *[pltpu.VMEM(operand.shape, operand.dtype) for operand in operands],
            rows,
            rows,
            rows,
            rows,
            pltpu.VMEM((copies, own, length), narrow),
            pltpu.VMEM((copies, own, lanes), wide),
            pltpu.VMEM((seqs * group, points), wide),
            pltpu.VMEM((seqs * group, points), wide),
            pltpu.VMEM((group, seqs, 2 * points), narrow),
            pltpu.VMEM((group, seqs, 2 * points), narrow),
            rows,
            rows,
            pltpu.VMEM((copies, own, length), narrow),
            pltpu.VMEM((2, own, length), narrow),
            pltpu.VMEM((2, own, length // 2), narrow),
            pltpu.VMEM((copies, own, lanes), wide),
            pltpu.VMEM((copies, own, lanes), wide),
            pltpu.SemaphoreType.DMA((len(operands),)),
            pltpu.SemaphoreType.DMA((3, cuts)),
            pltpu.SemaphoreType.DMA((3, cuts)),
            pltpu.SemaphoreType.DMA((6, copies)),
            pltpu.SemaphoreType.DMA((6, copies)),
            pltpu.SemaphoreType.REGULAR,
        ],
        compiler_params=pltpu.CompilerParams(
            collective_id=0, has_side_effects=True, vmem_limit_bytes=48 * 1024 * 1024
        ),
    )(*operands)
    return grad[None], grad_filter, grad_gain[0]


def solution(mesh):
    placed = (P("dp", "seq", None), P("dp", "seq", None), P(("seq", "dp"), None), P(("seq", "dp")))
    return jax.shard_map(
        shards,
        mesh=mesh,
        in_specs=placed,
        out_specs=(P("dp", "seq", None), P(("seq", "dp"), None), P(("seq", "dp"))),
        check_vma=False,
    )
```

```python
import functools
import math

import jax
import jax.numpy as jnp
import ml_dtypes
import numpy as np
from jax import lax
from jax.experimental import pallas as pl
from jax.experimental.pallas import tpu as pltpu
from jax.sharding import PartitionSpec as P

MESH = pl.DeviceIdType.MESH
lanes = 128
wide = jnp.float32
unroll = 4
narrow = jnp.bfloat16


def tables(sources, points):
    whole = 2 * sources * points
    half = np.arange(sources) + 0.5
    outer = 2.0 * np.pi * np.outer(half, np.arange(sources)) / (2 * sources)
    turn = 2.0 * np.pi * np.outer(half, np.arange(points)) / whole
    inner = 2.0 * np.pi * (np.outer(np.arange(points), np.arange(points)) % points) / points
    cos, sin = np.cos(inner), np.sin(inner)
    as_narrow = lambda table: table.astype(ml_dtypes.bfloat16)
    return (
        as_narrow(np.concatenate([np.cos(outer), -np.sin(outer)], 0)),
        as_narrow(np.block([[cos, -sin], [sin, cos]])),
        as_narrow(np.block([[cos, sin], [-sin, cos]])),
        as_narrow(2.0 / whole * np.concatenate([np.cos(outer).T, -np.sin(outer).T], 1)),
        np.stack([np.cos(turn), np.sin(turn)]).astype(np.float32),
    )


def kernel(
    seqs, copies, cuts, scale,
    values_hbm, cotangent_hbm, filter_hbm, gain_hbm, outer_hbm, inner_hbm, back_inner_hbm, back_outer_hbm, turn_hbm,
    grad_ref, grad_filter_ref, grad_gain_ref,
    values_ref, cotangent_ref, filter_ref, gain_ref, outer_ref, inner_ref, back_inner_ref, back_outer_ref, turn_ref,
    cot_out, val_out, cot_in, val_in, filters, gains, cot_wide, val_wide, cot_spec, filter_spec,
    grad_out, grad_in, part_out, part_in, passed_in, gain_out, gain_in,
    load_sem, send_sem, recv_sem, near_send_sem, near_recv_sem, ready_sem,
):
    me, mine = lax.axis_index("seq"), lax.axis_index("dp")
    points = values_ref.shape[0]
    group = cot_in.shape[1]
    own = filter_ref.shape[0]
    per_tile = lanes // group
    width = group // cuts
    shares = copies // cuts
    plane = 1 << (seqs.bit_length() // 2)
    columns = seqs // plane
    half = filter_ref.shape[1] // 2
    right, left = 1, copies - 1
    first = 1 - mine // shares

    def rows_of_cut(cut):
        return pl.ds(pl.multiple_of(lax.rem(first + cut, cuts) * width, width), width)

    def dp_at(step):
        return lax.rem(mine + step, copies)

    loads = {}
    for at, (name, src_ref, dst_ref) in enumerate(
        (
            ("cotangent", cotangent_hbm, cotangent_ref),
            ("filter", filter_hbm, filter_ref),
            ("gain", gain_hbm, gain_ref),
            ("values", values_hbm, values_ref),
            ("outer", outer_hbm, outer_ref),
            ("inner", inner_hbm, inner_ref),
            ("turn", turn_hbm, turn_ref),
            ("back_inner", back_inner_hbm, back_inner_ref),
            ("back_outer", back_outer_hbm, back_outer_ref),
        )
    ):
        loads[name] = pltpu.make_async_copy(src_ref, dst_ref, load_sem.at[at])
        loads[name].start()

    barrier = pltpu.get_barrier_semaphore()
    in_plane, in_column = lax.rem(me, plane), me // plane

    def column_peer(step):
        return lax.rem(in_column + step, columns) * plane + in_plane

    def greet_column(step, carry):
        pl.semaphore_signal(barrier, inc=1, device_id={"seq": column_peer(step)}, device_id_type=MESH)
        return carry

    def greet_plane(step, carry):
        peer = in_column * plane + lax.rem(in_plane + step, plane)
        pl.semaphore_signal(barrier, inc=1, device_id={"seq": peer}, device_id_type=MESH)
        return carry

    def tell_column(step, carry):
        pl.semaphore_signal(ready_sem, inc=1, device_id={"seq": column_peer(step)}, device_id_type=MESH)
        return carry

    lax.fori_loop(1, columns, greet_column, 0)
    lax.fori_loop(1, plane, greet_plane, 0)
    for step in range(1, copies):
        pl.semaphore_signal(barrier, inc=1, device_id={"dp": lax.rem(mine + step, copies)}, device_id_type=MESH)

    def turn_round(tokens_ref, rows_ref):
        def tile(at, carry):
            block = tokens_ref[:, pl.ds(pl.multiple_of(at * lanes, lanes), lanes)]
            rows_ref[pl.ds(at * per_tile, per_tile)] = block.T.reshape(per_tile, group, points)
            return carry

        lax.fori_loop(0, seqs // per_tile, tile, 0, unroll=2)

    def send(rows_ref, there_ref, which, cut):
        part = rows_of_cut(cut)

        def one(step, carry):
            peer = lax.rem(me + step * 49, seqs)
            pltpu.make_async_remote_copy(
                src_ref=rows_ref.at[peer, part],
                dst_ref=there_ref.at[me, part],
                send_sem=send_sem.at[which, cut],
                recv_sem=recv_sem.at[which, cut],
                device_id={"seq": peer},
                device_id_type=MESH,
            ).start()
            return carry

        lax.fori_loop(1, seqs, one, 0)
        there_ref[pl.ds(me, 1), part] = rows_ref[pl.ds(me, 1), part]

    def all_of(rows_ref, there_ref, which, cut):
        part = rows_of_cut(cut)
        return pltpu.make_async_remote_copy(
            src_ref=rows_ref.at[pl.ds(0, seqs - 1), part],
            dst_ref=there_ref.at[pl.ds(0, seqs - 1), part],
            send_sem=send_sem.at[which, cut],
            recv_sem=recv_sem.at[which, cut],
            device_id={"seq": lax.rem(me + 1, seqs)},
            device_id_type=MESH,
        )

    def near(which, step, src_ref, dst_ref):
        return pltpu.make_async_remote_copy(
            src_ref=src_ref,
            dst_ref=dst_ref,
            send_sem=near_send_sem.at[which, step],
            recv_sem=near_recv_sem.at[which, step],
            device_id={"dp": lax.rem(mine + step, copies)},
            device_id_type=MESH,
        )

    pl.semaphore_wait(barrier, plane + columns + copies - 3)
    lax.fori_loop(1, columns, tell_column, 0)
    loads["cotangent"].wait()
    turn_round(cotangent_ref, cot_out)
    loads["filter"].wait()
    loads["gain"].wait()
    filters[pl.ds(mine, 1)] = filter_ref[...][None]
    diagonal = lax.broadcasted_iota(jnp.int32, (own, own), 0) == lax.broadcasted_iota(jnp.int32, (own, own), 1)
    gain_square = jnp.where(diagonal, jnp.broadcast_to(gain_ref[...].astype(wide), (own, own)), 0.0)
    gains[pl.ds(mine, 1)] = jnp.broadcast_to(jnp.sum(gain_square, axis=1, keepdims=True), (own, lanes))[None]
    pl.semaphore_wait(ready_sem, columns - 1)

    filter_copies = [near(0, step, filter_ref, filters.at[mine]) for step in (right, left)]
    gain_copies = [near(1, step, gains.at[mine], gains.at[mine]) for step in range(1, copies)]
    filter_passes = []
    for step, start in ((right, 0), (left, half)):
        passed = filters.at[dp_at(copies - step), :, pl.ds(start, half)]
        filter_passes.append(near(4, step, passed, passed))
    send(cot_out, cot_in, 0, 0)
    for copy in filter_copies + gain_copies:
        copy.start()
    loads["values"].wait()
    turn_round(values_ref, val_out)
    send(val_out, val_in, 1, 0)
    for copy, onward in zip(filter_copies, filter_passes):
        copy.wait_recv()
        onward.start()
    for cut in range(1, cuts):
        send(cot_out, cot_in, 0, cut)
        send(val_out, val_in, 1, cut)

    for name in ("outer", "inner", "turn", "back_inner", "back_outer"):
        loads[name].wait()
    outer, inner = outer_ref[...], inner_ref[...]
    back_inner, back_outer = back_inner_ref[...], back_outer_ref[...]
    dot = functools.partial(jnp.dot, preferred_element_type=wide)

    def rows_of(wide_ref, channel):
        return wide_ref[pl.ds(channel, seqs, stride=group), :]

    def transform(first, second):
        cos, sin = turn_ref[0], turn_ref[1]
        both = dot(outer, jnp.concatenate([first.astype(narrow), second.astype(narrow)], 1))
        turned = []
        for at in range(2):
            real = both[:seqs, at * points : (at + 1) * points]
            imag = both[seqs:, at * points : (at + 1) * points]
            turned.append(
                jnp.concatenate([(real * cos + imag * sin).astype(narrow), (imag * cos - real * sin).astype(narrow)], 1)
            )
        return [dot(part, inner) for part in turned]

    def times_conj(first, second):
        first_real, first_imag = first[:, :points].astype(wide), first[:, points:].astype(wide)
        second_real, second_imag = second[:, :points].astype(wide), second[:, points:].astype(wide)
        return jnp.concatenate(
            [
                (first_real * second_real + first_imag * second_imag).astype(narrow),
                (first_real * second_imag - first_imag * second_real).astype(narrow),
            ],
            1,
        )

    def invert(first, second):
        cos, sin = turn_ref[0], turn_ref[1]
        turned = []
        for spec in (first, second):
            both = dot(spec, back_inner)
            real, imag = both[:, :points], both[:, points:]
            turned.append(
                jnp.concatenate([(real * cos - imag * sin).astype(narrow), (real * sin + imag * cos).astype(narrow)], 0)
            )
        both = dot(back_outer, jnp.concatenate(turned, 1))
        return both[:, :points], both[:, points:]

    for copy in filter_passes + gain_copies:
        copy.wait_recv()

    def widen_filter(at, carry):
        for copy in range(copies):
            val_wide[pl.ds(at * group + copy * own, own), :] = filters[
                copy, :, pl.ds(pl.multiple_of(at * points, points), points)
            ].astype(wide)
        return carry

    lax.fori_loop(0, seqs, widen_filter, 0, unroll=4)

    def filter_pair(pair, carry):
        at = pair * 2
        specs = transform(rows_of(val_wide, at), rows_of(val_wide, at + 1))
        for offset in range(2):
            filter_spec[at + offset] = specs[offset].astype(narrow)
        return carry

    lax.fori_loop(0, group // 2, filter_pair, 0, unroll=unroll)

    def grad_pair(pair, carry):
        at = pair * 2
        rows = rows_of(cot_wide, at), rows_of(cot_wide, at + 1)
        specs = transform(*rows)
        lags = []
        for offset in range(2):
            spec = specs[offset].astype(narrow)
            cot_spec[at + offset] = spec
            lags.append(times_conj(filter_spec[at + offset], spec))
        signals = invert(*lags)
        for offset in range(2):
            channel = at + offset
            gain = gains[channel // own, pl.ds(lax.rem(channel, own), 1), :]
            cot_wide[pl.ds(channel, seqs, stride=group), :] = signals[offset] + gain * rows[offset]
        return carry

    def cross_pair(pair, carry):
        at = pair * 2
        specs = transform(rows_of(val_wide, at), rows_of(val_wide, at + 1))
        parts = [times_conj(specs[offset].astype(narrow), cot_spec[at + offset]) for offset in range(2)]
        signals = invert(*parts)
        for offset in range(2):
            val_wide[pl.ds(at + offset, seqs, stride=group), :] = signals[offset]
        return carry

    part_copies = {}
    pass_copies = []
    for step, start in ((right, 0), (left, half)):
        side = 0 if step == right else 1
        part_copies[step] = near(2, step, part_out.at[dp_at(step)], part_in.at[side])
        pass_copies.append(near(5, step, part_out.at[dp_at(2), :, pl.ds(start, half)], passed_in.at[side]))
    gain_sums = [near(3, step, gain_out.at[dp_at(step)], gain_in.at[mine]) for step in range(1, copies)]

    def hand_over(step):
        side = 0 if step == right else 1
        there = dp_at(step)
        pass_copies[side].wait_recv()

        def add(at, carry):
            here = pl.multiple_of(at * points, points)
            where = pl.ds(side * half + here, points)
            sent_on = part_out[there, :, where].astype(wide) + passed_in[side, :, pl.ds(here, points)].astype(wide)
            part_out[there, :, where] = sent_on.astype(narrow)
            return carry

        lax.fori_loop(0, seqs // 2, add, 0, unroll=min(4, seqs // 2))
        part_copies[step].start()

    even = lax.rem(mine, 2) == 0
    passing = False

    for cut in range(cuts):
        part = rows_of_cut(cut)
        begin = lax.rem(first + cut, cuts)

        def rows_at(at):
            return pl.ds(pl.multiple_of(at * group + begin * width, width), width)

        all_of(cot_out, cot_in, 0, cut).wait_recv()

        def widen_cot(at, carry):
            cot_wide[rows_at(at), :] = cot_in[at, part].astype(wide)
            return carry

        lax.fori_loop(0, seqs, widen_cot, 0, unroll=4)
        lax.fori_loop(0, width // 2, lambda pair, carry: grad_pair(begin * (width // 2) + pair, carry), 0, unroll=unroll)

        def pack_grad(at, carry):
            grad_out[at, part] = cot_wide[rows_at(at), :].astype(narrow)
            return carry

        lax.fori_loop(0, seqs, pack_grad, 0, unroll=4)
        send(grad_out, grad_in, 2, cut)

        all_of(val_out, val_in, 1, cut).wait_recv()

        def widen_val(at, total):
            block = val_in[at, part].astype(wide)
            val_wide[rows_at(at), :] = block
            return total + block * cot_in[at, part].astype(wide)

        total = lax.fori_loop(0, seqs, widen_val, jnp.zeros((width, points), wide), unroll=4)
        gain_out[pl.ds(begin * shares, shares)] = total.reshape(shares, own, points)
        if cut == 1:
            pl.when(even)(lambda: hand_over(left))
            pl.when(jnp.logical_not(even))(lambda: hand_over(right))

        away = lax.rem(mine, 2) * 2
        for share in (dp_at(2), dp_at(left - away)) if cut == 0 else (dp_at(right + away), mine):
            begin_pair = share * (own // 2)
            lax.fori_loop(0, own // 2, lambda pair, carry: cross_pair(begin_pair + pair, carry), 0, unroll=unroll)

            def pack_part(at, carry):
                part_out[share, :, pl.ds(pl.multiple_of(at * points, points), points)] = val_wide[
                    pl.ds(pl.multiple_of(at * group + share * own, own), own), :
                ].astype(narrow)
                return carry

            lax.fori_loop(0, seqs, pack_part, 0, unroll=4)
            if share is not mine and cut == 1:
                pl.when(even)(lambda: hand_over(right))
                pl.when(jnp.logical_not(even))(lambda: hand_over(left))
            elif cut == 0 and not passing:
                passing = True
                for copy in pass_copies:
                    copy.start()
    for copy in gain_sums:
        copy.start()
    gain_in[pl.ds(mine, 1)] = gain_out[pl.ds(mine, 1)]

    def place(at, carry):
        block = grad_in[pl.ds(at * per_tile, per_tile)].reshape(lanes, points)
        grad_ref[:, pl.ds(pl.multiple_of(at * lanes, lanes), lanes)] = block.T
        return carry

    for cut in range(cuts):
        all_of(grad_out, grad_in, 2, cut).wait_recv()
    lax.fori_loop(0, seqs // per_tile, place, 0, unroll=2)

    for copy in [*part_copies.values(), *gain_sums]:
        copy.wait_recv()

    def sum_parts(at, carry):
        where = pl.ds(pl.multiple_of(at * points, points), points)
        total = part_out[mine, :, where].astype(wide) + part_in[0, :, where].astype(wide)
        grad_filter_ref[:, where] = (total + part_in[1, :, where].astype(wide)) * scale
        return carry

    lax.fori_loop(0, seqs, sum_parts, 0, unroll=4)
    total = gain_in[0]
    for copy in range(1, copies):
        total = total + gain_in[copy]
    total = jnp.broadcast_to(jnp.sum(total, axis=1, keepdims=True) * scale, (own, own))
    grad_gain_ref[...] = jnp.sum(jnp.where(diagonal, total, 0.0), axis=0, keepdims=True)

    for copy in filter_copies + gain_copies + filter_passes + pass_copies + [*part_copies.values(), *gain_sums]:
        copy.wait_send()
    for cut in range(cuts):
        all_of(cot_out, cot_in, 0, cut).wait_send()
        all_of(val_out, val_in, 1, cut).wait_send()
        all_of(grad_out, grad_in, 2, cut).wait_send()


def shards(values, cotangent, long_filter, bypass):
    seqs, copies = lax.axis_size("seq"), lax.axis_size("dp")
    points, channels = values.shape[1:]
    group = channels // seqs
    own, length = long_filter.shape
    scale = 1.0 / math.sqrt(copies * length)
    consts = tables(seqs, points)
    vmem, hbm = pl.BlockSpec(memory_space=pltpu.VMEM), pl.BlockSpec(memory_space=pltpu.HBM)
    operands = (values[0], cotangent[0], long_filter, bypass[None], *consts)
    operands = [pltpu.with_memory_space_constraint(operand, pltpu.HBM) for operand in operands]
    cuts = 2
    rows = pltpu.VMEM((seqs, group, points), narrow)
    grad, grad_filter, grad_gain = pl.pallas_call(
        functools.partial(kernel, seqs, copies, cuts, scale),
        out_shape=(
            pltpu.VMEM((points, channels), narrow),
            pltpu.VMEM((own, length), wide),
            pltpu.VMEM((1, own), wide),
        ),
        in_specs=[hbm] * len(operands),
        out_specs=(vmem,) * 3,
        scratch_shapes=[
            *[pltpu.VMEM(operand.shape, operand.dtype) for operand in operands],
            rows,
            rows,
            rows,
            rows,
            pltpu.VMEM((copies, own, length), narrow),
            pltpu.VMEM((copies, own, lanes), wide),
            pltpu.VMEM((seqs * group, points), wide),
            pltpu.VMEM((seqs * group, points), wide),
            pltpu.VMEM((group, seqs, 2 * points), narrow),
            pltpu.VMEM((group, seqs, 2 * points), narrow),
            rows,
            rows,
            pltpu.VMEM((copies, own, length), narrow),
            pltpu.VMEM((2, own, length), narrow),
            pltpu.VMEM((2, own, length // 2), narrow),
            pltpu.VMEM((copies, own, lanes), wide),
            pltpu.VMEM((copies, own, lanes), wide),
            pltpu.SemaphoreType.DMA((len(operands),)),
            pltpu.SemaphoreType.DMA((3, cuts)),
            pltpu.SemaphoreType.DMA((3, cuts)),
            pltpu.SemaphoreType.DMA((6, copies)),
            pltpu.SemaphoreType.DMA((6, copies)),
            pltpu.SemaphoreType.REGULAR,
        ],
        compiler_params=pltpu.CompilerParams(
            collective_id=0, has_side_effects=True, vmem_limit_bytes=48 * 1024 * 1024
        ),
    )(*operands)
    return grad[None], grad_filter, grad_gain[0]


def solution(mesh):
    placed = (P("dp", "seq", None), P("dp", "seq", None), P(("seq", "dp"), None), P(("seq", "dp")))
    return jax.shard_map(
        shards,
        mesh=mesh,
        in_specs=placed,
        out_specs=(P("dp", "seq", None), P(("seq", "dp"), None), P(("seq", "dp"))),
        check_vma=False,
    )
```

```python
import functools
import math

import jax
import jax.numpy as jnp
import ml_dtypes
import numpy as np
from jax import lax
from jax.experimental import pallas as pl
from jax.experimental.pallas import tpu as pltpu
from jax.sharding import PartitionSpec as P

MESH = pl.DeviceIdType.MESH
lanes = 128
wide = jnp.float32
unroll = 8
narrow = jnp.bfloat16


def tables(sources, points):
    whole = 2 * sources * points
    half = np.arange(sources) + 0.5
    outer = 2.0 * np.pi * np.outer(half, np.arange(sources)) / (2 * sources)
    turn = 2.0 * np.pi * np.outer(half, np.arange(points)) / whole
    inner = 2.0 * np.pi * (np.outer(np.arange(points), np.arange(points)) % points) / points
    cos, sin = np.cos(inner), np.sin(inner)
    as_narrow = lambda table: table.astype(ml_dtypes.bfloat16)
    return (
        as_narrow(np.concatenate([np.cos(outer), -np.sin(outer)], 0)),
        as_narrow(np.block([[cos, -sin], [sin, cos]])),
        as_narrow(np.block([[cos, sin], [-sin, cos]])),
        as_narrow(2.0 / whole * np.concatenate([np.cos(outer).T, -np.sin(outer).T], 1)),
        np.stack([np.cos(turn), np.sin(turn)]).astype(np.float32),
    )


def kernel(
    seqs, copies, cuts, scale,
    values_hbm, cotangent_hbm, filter_hbm, gain_hbm, outer_hbm, inner_hbm, back_inner_hbm, back_outer_hbm, turn_hbm,
    grad_ref, grad_filter_ref, grad_gain_ref,
    values_ref, cotangent_ref, filter_ref, gain_ref, outer_ref, inner_ref, back_inner_ref, back_outer_ref, turn_ref,
    cot_out, val_out, cot_in, val_in, filters, gains, cot_wide, val_wide, cot_spec, filter_spec,
    grad_out, grad_in, part_out, part_in, passed_in, gain_out, gain_in,
    load_sem, send_sem, recv_sem, near_send_sem, near_recv_sem, ready_sem,
):
    me, mine = lax.axis_index("seq"), lax.axis_index("dp")
    points = values_ref.shape[0]
    group = cot_in.shape[1]
    own = filter_ref.shape[0]
    per_tile = lanes // group
    width = group // cuts
    shares = copies // cuts
    plane = 1 << (seqs.bit_length() // 2)
    columns = seqs // plane
    half = filter_ref.shape[1] // 2
    right, left = 1, copies - 1
    first = 1 - mine // shares

    def rows_of_cut(cut):
        return pl.ds(pl.multiple_of(lax.rem(first + cut, cuts) * width, width), width)

    def dp_at(step):
        return lax.rem(mine + step, copies)

    loads = {}
    for at, (name, src_ref, dst_ref) in enumerate(
        (
            ("cotangent", cotangent_hbm, cotangent_ref),
            ("filter", filter_hbm, filter_ref),
            ("gain", gain_hbm, gain_ref),
            ("values", values_hbm, values_ref),
            ("outer", outer_hbm, outer_ref),
            ("inner", inner_hbm, inner_ref),
            ("turn", turn_hbm, turn_ref),
            ("back_inner", back_inner_hbm, back_inner_ref),
            ("back_outer", back_outer_hbm, back_outer_ref),
        )
    ):
        loads[name] = pltpu.make_async_copy(src_ref, dst_ref, load_sem.at[at])
        loads[name].start()

    barrier = pltpu.get_barrier_semaphore()
    in_plane, in_column = lax.rem(me, plane), me // plane

    def column_peer(step):
        return lax.rem(in_column + step, columns) * plane + in_plane

    def greet_column(step, carry):
        pl.semaphore_signal(barrier, inc=1, device_id={"seq": column_peer(step)}, device_id_type=MESH)
        return carry

    def greet_plane(step, carry):
        peer = in_column * plane + lax.rem(in_plane + step, plane)
        pl.semaphore_signal(barrier, inc=1, device_id={"seq": peer}, device_id_type=MESH)
        return carry

    def tell_column(step, carry):
        pl.semaphore_signal(ready_sem, inc=1, device_id={"seq": column_peer(step)}, device_id_type=MESH)
        return carry

    lax.fori_loop(1, columns, greet_column, 0)
    lax.fori_loop(1, plane, greet_plane, 0)
    for step in range(1, copies):
        pl.semaphore_signal(barrier, inc=1, device_id={"dp": lax.rem(mine + step, copies)}, device_id_type=MESH)

    def turn_round(tokens_ref, rows_ref):
        def tile(at, carry):
            block = tokens_ref[:, pl.ds(pl.multiple_of(at * lanes, lanes), lanes)]
            rows_ref[pl.ds(at * per_tile, per_tile)] = block.T.reshape(per_tile, group, points)
            return carry

        lax.fori_loop(0, seqs // per_tile, tile, 0, unroll=2)

    def send(rows_ref, there_ref, which, cut):
        part = rows_of_cut(cut)

        def one(step, carry):
            peer = lax.rem(me + step * (49 + 30 * lax.rem(me, 2)), seqs)
            pltpu.make_async_remote_copy(
                src_ref=rows_ref.at[peer, part],
                dst_ref=there_ref.at[me, part],
                send_sem=send_sem.at[which, cut],
                recv_sem=recv_sem.at[which, cut],
                device_id={"seq": peer},
                device_id_type=MESH,
            ).start()
            return carry

        lax.fori_loop(1, seqs, one, 0)
        there_ref[pl.ds(me, 1), part] = rows_ref[pl.ds(me, 1), part]

    def all_of(rows_ref, there_ref, which, cut):
        part = rows_of_cut(cut)
        return pltpu.make_async_remote_copy(
            src_ref=rows_ref.at[pl.ds(0, seqs - 1), part],
            dst_ref=there_ref.at[pl.ds(0, seqs - 1), part],
            send_sem=send_sem.at[which, cut],
            recv_sem=recv_sem.at[which, cut],
            device_id={"seq": lax.rem(me + 1, seqs)},
            device_id_type=MESH,
        )

    def near(which, step, src_ref, dst_ref):
        return pltpu.make_async_remote_copy(
            src_ref=src_ref,
            dst_ref=dst_ref,
            send_sem=near_send_sem.at[which, step],
            recv_sem=near_recv_sem.at[which, step],
            device_id={"dp": lax.rem(mine + step, copies)},
            device_id_type=MESH,
        )

    pl.semaphore_wait(barrier, plane + columns + copies - 3)
    lax.fori_loop(1, columns, tell_column, 0)
    loads["cotangent"].wait()
    turn_round(cotangent_ref, cot_out)
    loads["filter"].wait()
    loads["gain"].wait()
    filters[pl.ds(mine, 1)] = filter_ref[...][None]
    diagonal = lax.broadcasted_iota(jnp.int32, (own, own), 0) == lax.broadcasted_iota(jnp.int32, (own, own), 1)
    gain_square = jnp.where(diagonal, jnp.broadcast_to(gain_ref[...].astype(wide), (own, own)), 0.0)
    gains[pl.ds(mine, 1)] = jnp.broadcast_to(jnp.sum(gain_square, axis=1, keepdims=True), (own, lanes))[None]
    pl.semaphore_wait(ready_sem, columns - 1)

    filter_copies = [near(0, step, filter_ref, filters.at[mine]) for step in (right, left)]
    gain_copies = [near(1, step, gains.at[mine], gains.at[mine]) for step in range(1, copies)]
    filter_passes = []
    for step, start in ((right, 0), (left, half)):
        passed = filters.at[dp_at(copies - step), :, pl.ds(start, half)]
        filter_passes.append(near(4, step, passed, passed))
    send(cot_out, cot_in, 0, 0)
    for copy in filter_copies + gain_copies:
        copy.start()
    loads["values"].wait()
    turn_round(values_ref, val_out)
    send(val_out, val_in, 1, 0)
    for copy, onward in zip(filter_copies, filter_passes):
        copy.wait_recv()
        onward.start()
    for cut in range(1, cuts):
        send(cot_out, cot_in, 0, cut)
        send(val_out, val_in, 1, cut)

    for name in ("outer", "inner", "turn", "back_inner", "back_outer"):
        loads[name].wait()
    outer, inner = outer_ref[...], inner_ref[...]
    back_inner, back_outer = back_inner_ref[...], back_outer_ref[...]
    dot = functools.partial(jnp.dot, preferred_element_type=wide)

    def rows_of(wide_ref, channel):
        return wide_ref[pl.ds(channel, seqs, stride=group), :]

    def transform(first, second):
        cos, sin = turn_ref[0], turn_ref[1]
        both = dot(outer, jnp.concatenate([first.astype(narrow), second.astype(narrow)], 1))
        turned = []
        for at in range(2):
            real = both[:seqs, at * points : (at + 1) * points]
            imag = both[seqs:, at * points : (at + 1) * points]
            turned.append(
                jnp.concatenate([(real * cos + imag * sin).astype(narrow), (imag * cos - real * sin).astype(narrow)], 1)
            )
        return [dot(part, inner) for part in turned]

    def times_conj(first, second):
        first_real, first_imag = first[:, :points].astype(wide), first[:, points:].astype(wide)
        second_real, second_imag = second[:, :points].astype(wide), second[:, points:].astype(wide)
        return jnp.concatenate(
            [
                (first_real * second_real + first_imag * second_imag).astype(narrow),
                (first_real * second_imag - first_imag * second_real).astype(narrow),
            ],
            1,
        )

    def invert(first, second):
        cos, sin = turn_ref[0], turn_ref[1]
        turned = []
        for spec in (first, second):
            both = dot(spec, back_inner)
            real, imag = both[:, :points], both[:, points:]
            turned.append(
                jnp.concatenate([(real * cos - imag * sin).astype(narrow), (real * sin + imag * cos).astype(narrow)], 0)
            )
        both = dot(back_outer, jnp.concatenate(turned, 1))
        return both[:, :points], both[:, points:]

    for copy in filter_passes + gain_copies:
        copy.wait_recv()

    def widen_filter(at, carry):
        for copy in range(copies):
            val_wide[pl.ds(at * group + copy * own, own), :] = filters[
                copy, :, pl.ds(pl.multiple_of(at * points, points), points)
            ].astype(wide)
        return carry

    lax.fori_loop(0, seqs, widen_filter, 0, unroll=4)

    def filter_pair(pair, carry):
        at = pair * 2
        specs = transform(rows_of(val_wide, at), rows_of(val_wide, at + 1))
        for offset in range(2):
            filter_spec[at + offset] = specs[offset].astype(narrow)
        return carry

    lax.fori_loop(0, group // 2, filter_pair, 0, unroll=unroll)

    def grad_pair(pair, carry):
        at = pair * 2
        rows = rows_of(cot_wide, at), rows_of(cot_wide, at + 1)
        specs = transform(*rows)
        lags = []
        for offset in range(2):
            spec = specs[offset].astype(narrow)
            cot_spec[at + offset] = spec
            lags.append(times_conj(filter_spec[at + offset], spec))
        signals = invert(*lags)
        for offset in range(2):
            channel = at + offset
            gain = gains[channel // own, pl.ds(lax.rem(channel, own), 1), :]
            cot_wide[pl.ds(channel, seqs, stride=group), :] = signals[offset] + gain * rows[offset]
        return carry

    def cross_pair(pair, carry):
        at = pair * 2
        specs = transform(rows_of(val_wide, at), rows_of(val_wide, at + 1))
        parts = [times_conj(specs[offset].astype(narrow), cot_spec[at + offset]) for offset in range(2)]
        signals = invert(*parts)
        for offset in range(2):
            val_wide[pl.ds(at + offset, seqs, stride=group), :] = signals[offset]
        return carry

    part_copies = {}
    pass_copies = []
    for step, start in ((right, 0), (left, half)):
        side = 0 if step == right else 1
        part_copies[step] = near(2, step, part_out.at[dp_at(step)], part_in.at[side])
        pass_copies.append(near(5, step, part_out.at[dp_at(2), :, pl.ds(start, half)], passed_in.at[side]))
    gain_sums = [near(3, step, gain_out.at[dp_at(step)], gain_in.at[mine]) for step in range(1, copies)]

    def hand_over(step):
        side = 0 if step == right else 1
        there = dp_at(step)
        pass_copies[side].wait_recv()

        def add(at, carry):
            here = pl.multiple_of(at * points, points)
            where = pl.ds(side * half + here, points)
            sent_on = part_out[there, :, where].astype(wide) + passed_in[side, :, pl.ds(here, points)].astype(wide)
            part_out[there, :, where] = sent_on.astype(narrow)
            return carry

        lax.fori_loop(0, seqs // 2, add, 0, unroll=min(4, seqs // 2))
        part_copies[step].start()

    even = lax.rem(mine, 2) == 0
    passing = False

    for cut in range(cuts):
        part = rows_of_cut(cut)
        begin = lax.rem(first + cut, cuts)

        def rows_at(at):
            return pl.ds(pl.multiple_of(at * group + begin * width, width), width)

        all_of(cot_out, cot_in, 0, cut).wait_recv()

        def widen_cot(at, carry):
            cot_wide[rows_at(at), :] = cot_in[at, part].astype(wide)
            return carry

        lax.fori_loop(0, seqs, widen_cot, 0, unroll=4)
        lax.fori_loop(0, width // 2, lambda pair, carry: grad_pair(begin * (width // 2) + pair, carry), 0, unroll=unroll)

        def pack_grad(at, carry):
            grad_out[at, part] = cot_wide[rows_at(at), :].astype(narrow)
            return carry

        lax.fori_loop(0, seqs, pack_grad, 0, unroll=4)
        send(grad_out, grad_in, 2, cut)

        all_of(val_out, val_in, 1, cut).wait_recv()

        def widen_val(at, total):
            block = val_in[at, part].astype(wide)
            val_wide[rows_at(at), :] = block
            return total + block * cot_in[at, part].astype(wide)

        total = lax.fori_loop(0, seqs, widen_val, jnp.zeros((width, points), wide), unroll=4)
        gain_out[pl.ds(begin * shares, shares)] = total.reshape(shares, own, points)
        if cut == 1:
            pl.when(even)(lambda: hand_over(left))
            pl.when(jnp.logical_not(even))(lambda: hand_over(right))

        away = lax.rem(mine, 2) * 2
        for share in (dp_at(2), dp_at(left - away)) if cut == 0 else (dp_at(right + away), mine):
            begin_pair = share * (own // 2)
            lax.fori_loop(0, own // 2, lambda pair, carry: cross_pair(begin_pair + pair, carry), 0, unroll=own // 2)

            def pack_part(at, carry):
                part_out[share, :, pl.ds(pl.multiple_of(at * points, points), points)] = val_wide[
                    pl.ds(pl.multiple_of(at * group + share * own, own), own), :
                ].astype(narrow)
                return carry

            lax.fori_loop(0, seqs, pack_part, 0, unroll=4)
            if share is not mine and cut == 1:
                pl.when(even)(lambda: hand_over(right))
                pl.when(jnp.logical_not(even))(lambda: hand_over(left))
            elif cut == 0 and not passing:
                passing = True
                for copy in pass_copies:
                    copy.start()
    for copy in gain_sums:
        copy.start()
    gain_in[pl.ds(mine, 1)] = gain_out[pl.ds(mine, 1)]

    def place(at, carry):
        block = grad_in[pl.ds(at * per_tile, per_tile)].reshape(lanes, points)
        grad_ref[:, pl.ds(pl.multiple_of(at * lanes, lanes), lanes)] = block.T
        return carry

    for cut in range(cuts):
        all_of(grad_out, grad_in, 2, cut).wait_recv()
    lax.fori_loop(0, seqs // per_tile, place, 0, unroll=2)

    for copy in [*part_copies.values(), *gain_sums]:
        copy.wait_recv()

    def sum_parts(at, carry):
        where = pl.ds(pl.multiple_of(at * points, points), points)
        total = part_out[mine, :, where].astype(wide) + part_in[0, :, where].astype(wide)
        grad_filter_ref[:, where] = (total + part_in[1, :, where].astype(wide)) * scale
        return carry

    lax.fori_loop(0, seqs, sum_parts, 0, unroll=4)
    total = gain_in[0]
    for copy in range(1, copies):
        total = total + gain_in[copy]
    total = jnp.broadcast_to(jnp.sum(total, axis=1, keepdims=True) * scale, (own, own))
    grad_gain_ref[...] = jnp.sum(jnp.where(diagonal, total, 0.0), axis=0, keepdims=True)

    for copy in filter_copies + gain_copies + filter_passes + pass_copies + [*part_copies.values(), *gain_sums]:
        copy.wait_send()
    for cut in range(cuts):
        all_of(cot_out, cot_in, 0, cut).wait_send()
        all_of(val_out, val_in, 1, cut).wait_send()
        all_of(grad_out, grad_in, 2, cut).wait_send()


def shards(values, cotangent, long_filter, bypass):
    seqs, copies = lax.axis_size("seq"), lax.axis_size("dp")
    points, channels = values.shape[1:]
    group = channels // seqs
    own, length = long_filter.shape
    scale = 1.0 / math.sqrt(copies * length)
    consts = tables(seqs, points)
    vmem, hbm = pl.BlockSpec(memory_space=pltpu.VMEM), pl.BlockSpec(memory_space=pltpu.HBM)
    operands = (values[0], cotangent[0], long_filter, bypass[None], *consts)
    operands = [pltpu.with_memory_space_constraint(operand, pltpu.HBM) for operand in operands]
    cuts = 2
    rows = pltpu.VMEM((seqs, group, points), narrow)
    grad, grad_filter, grad_gain = pl.pallas_call(
        functools.partial(kernel, seqs, copies, cuts, scale),
        out_shape=(
            pltpu.VMEM((points, channels), narrow),
            pltpu.VMEM((own, length), wide),
            pltpu.VMEM((1, own), wide),
        ),
        in_specs=[hbm] * len(operands),
        out_specs=(vmem,) * 3,
        scratch_shapes=[
            *[pltpu.VMEM(operand.shape, operand.dtype) for operand in operands],
            rows,
            rows,
            rows,
            rows,
            pltpu.VMEM((copies, own, length), narrow),
            pltpu.VMEM((copies, own, lanes), wide),
            pltpu.VMEM((seqs * group, points), wide),
            pltpu.VMEM((seqs * group, points), wide),
            pltpu.VMEM((group, seqs, 2 * points), narrow),
            pltpu.VMEM((group, seqs, 2 * points), narrow),
            rows,
            rows,
            pltpu.VMEM((copies, own, length), narrow),
            pltpu.VMEM((2, own, length), narrow),
            pltpu.VMEM((2, own, length // 2), narrow),
            pltpu.VMEM((copies, own, lanes), wide),
            pltpu.VMEM((copies, own, lanes), wide),
            pltpu.SemaphoreType.DMA((len(operands),)),
            pltpu.SemaphoreType.DMA((3, cuts)),
            pltpu.SemaphoreType.DMA((3, cuts)),
            pltpu.SemaphoreType.DMA((6, copies)),
            pltpu.SemaphoreType.DMA((6, copies)),
            pltpu.SemaphoreType.REGULAR,
        ],
        compiler_params=pltpu.CompilerParams(
            collective_id=0, has_side_effects=True, vmem_limit_bytes=48 * 1024 * 1024
        ),
    )(*operands)
    return grad[None], grad_filter, grad_gain[0]


def solution(mesh):
    placed = (P("dp", "seq", None), P("dp", "seq", None), P(("seq", "dp"), None), P(("seq", "dp")))
    return jax.shard_map(
        shards,
        mesh=mesh,
        in_specs=placed,
        out_specs=(P("dp", "seq", None), P(("seq", "dp"), None), P(("seq", "dp"))),
        check_vma=False,
    )
```
